32 devices in a mesh: samp: 8 (over y, x, core), var: 4 (over z).
Axes of the slice: x: 2, y: 2, z: 4, core: 2. Of those that a mesh axis runs over, the one named last changes fastest.
Arguments:
- genotypes: int32 [8192, 4096], P('samp', 'var'), may hold values from 0 to 2
- observed: int32 [8192, 4096], P('samp', 'var'), may hold values from 0 to 1, as said below
- proportions: float32 [10, 8192], P(None, 'samp'), may hold values from 0 to 1, as said below
- frequencies: float32 [10, 4096], P(None, ('samp', 'var')), may hold values from 0.02 to 0.98
Outputs:
- mixture: float32 [10, 8192], P(None, 'samp')
- alleles: float32 [10, 4096], P(None, 'var')
The draws below stay inside these ranges and needn't reach their ends.
Inputs may be any that keep to these rules, and one draw needn't show every extreme that they name: Every sample is observed at 256 or more variants and every variant at 512 or more samples. Each sample's 10 proportions are positive and sum to one.
All inputs are finite; a program needn't handle non-finite values.
Results may differ from the reference program's by a relative error of at most 0.0003.
Values sent between devices are 32-bit elements; how exact they have to be, the bound alone decides.
No kernel may reach another device: no remote copies, remote signals or barrier semaphores. Data moves between devices by JAX's collectives and lax.ppermute only.
A program may use at most 128 MiB of HBM per device.

```python
import jax
import jax.numpy as jnp
from jax import lax

K = 10
N_DEV = 1024
STEPS = 2
SAMPLES = 8192
M = 4096


def draw_observed(key, part):
    key_cells, key_rows, key_cols = jax.random.split(jax.random.fold_in(key, 11), 3)
    missing_draw = jax.random.randint(key_cells, (SAMPLES, M), 0, 16)
    row_shift = jax.random.randint(key_rows, (SAMPLES, 1), 0, 16)
    col_shift = jax.random.randint(key_cols, (1, M), 0, 16)
    row_index = lax.broadcasted_iota(jnp.int32, (SAMPLES, 1), 0)
    col_index = lax.broadcasted_iota(jnp.int32, (1, M), 1)
    kept = (missing_draw != 0) | ((col_index + row_shift) % 16 == 0) | ((row_index + col_shift) % 16 == 0)
    return kept.astype(jnp.int32)


def draw_proportions(key, part):
    inner = jax.random.fold_in(key, 23)
    raw_logs = jax.random.uniform(inner, (K, SAMPLES), jnp.float32, -2.0, 2.0)
    weights = jnp.exp(raw_logs)
    return weights / jnp.sum(weights, axis=0, keepdims=True)


def touch_ends(entries, rng, smallest, top_value):
    dims = entries.shape
    spot = [jax.random.randint(jax.random.fold_in(rng, axis), (), 0, dims[axis]) for axis in range(len(dims))]
    entries = entries.at[tuple(spot)].set(smallest)
    longest = dims.index(max(dims))
    spot[longest] = (spot[longest] + 1) % dims[longest]
    return entries.at[tuple(spot)].set(top_value)


def level_of(own_key, shape, cuts, low, high):
    def one(position, shards_of):
        draws = jax.random.uniform(jax.random.fold_in(jax.random.fold_in(own_key, 6), position), (shards_of,), jnp.float32, low / len(cuts), high / len(cuts))
        return jnp.repeat(jnp.exp(draws), shape[position] // shards_of).reshape((-1,) + (1,) * (len(shape) - position - 1))

    gain = one(*cuts[0])
    for cut in cuts[1:]:
        gain = gain * one(*cut)
    return gain


def setup_inputs(seed: int = 0) -> dict:
    key_list = jax.random.split(jax.random.key(seed), 5)
    genotypes = touch_ends(jax.random.randint(key_list[0], (SAMPLES, M), 0, 3), jax.random.fold_in(key_list[0], 1), 0, 2).astype(jnp.int32)
    observed = draw_observed(jax.random.fold_in(key_list[4], 71), 0)
    proportions = draw_proportions(jax.random.fold_in(key_list[4], 71), 0)
    frequencies = jnp.clip(0.02 + 0.96000002 * jax.random.uniform(key_list[3], (K, M), jnp.float32) ** level_of(key_list[3], (K, M), ((1, 32),), -0.2, 0.2), 0.02, 0.98)
    return dict(genotypes=genotypes, observed=observed, proportions=proportions, frequencies=frequencies)


CLIP_LOW = 1e-05
NORM_EPS = 1e-10
EXACT = lax.Precision.HIGHEST

def clip_unit(values):
    return jnp.clip(values, CLIP_LOW, 1.0 - CLIP_LOW)

def tidy_mixture(mixture):
    clipped = clip_unit(mixture)
    return clipped / lax.optimization_barrier(jnp.sum(clipped, axis=0, keepdims=True))

def step_size(first, second):
    return jnp.maximum(1.0, jnp.sqrt(first / (second + NORM_EPS)))

def expectation_step(genotypes, observed, twice_observed, mixture, alleles):
    block_count = SAMPLES // N_DEV
    geno_blocks = genotypes.reshape(block_count, N_DEV, M)
    seen_blocks = observed.reshape(block_count, N_DEV, M)
    mix_blocks = jnp.transpose(mixture.reshape(K, block_count, N_DEV), (1, 0, 2))

    def visit_block(running, block_data):
        geno_block, seen_block, mix_block = block_data
        geno_vals = geno_block.astype(jnp.float32)
        seen_vals = seen_block.astype(jnp.float32)
        expected = lax.dot_general(mix_block, alleles, (((0,), (0,)), ((), ())), precision=EXACT, preferred_element_type=jnp.float32)
        ratio_alt = seen_vals * geno_vals / expected
        ratio_ref = seen_vals * (2.0 - geno_vals) / (1.0 - expected)
        prop_terms = lax.dot_general(alleles, ratio_alt, (((1,), (1,)), ((), ())), precision=EXACT, preferred_element_type=jnp.float32)
        prop_terms = prop_terms + lax.dot_general(1.0 - alleles, ratio_ref, (((1,), (1,)), ((), ())), precision=EXACT, preferred_element_type=jnp.float32)
        alt_terms = lax.dot_general(mix_block, ratio_alt, (((1,), (0,)), ((), ())), precision=EXACT, preferred_element_type=jnp.float32)
        ref_terms = lax.dot_general(mix_block, ratio_ref, (((1,), (0,)), ((), ())), precision=EXACT, preferred_element_type=jnp.float32)
        return ((running[0] + alt_terms, running[1] + ref_terms), prop_terms)
    zeros_start = jnp.zeros((K, M), jnp.float32)
    sums_pair, prop_blocks = lax.scan(visit_block, (zeros_start, zeros_start), (geno_blocks, seen_blocks, mix_blocks))
    alt_sums, ref_sums = sums_pair
    prop_sums = jnp.transpose(prop_blocks, (1, 0, 2)).reshape(K, SAMPLES)
    next_mixture = clip_unit(mixture * prop_sums / twice_observed)
    weighted = alleles * alt_sums
    next_alleles = clip_unit(weighted / (weighted + (1.0 - alleles) * ref_sums))
    return (next_mixture, next_alleles)

def reference(genotypes, observed, proportions, frequencies):
    twice_observed = 2.0 * lax.optimization_barrier(jnp.sum(observed, axis=1)).astype(jnp.float32)[None, :]
    mixture, alleles = (proportions, frequencies)
    for repeat in range(STEPS):
        mixture_one, alleles_one = expectation_step(genotypes, observed, twice_observed, mixture, alleles)
        mixture_two, alleles_two = expectation_step(genotypes, observed, twice_observed, mixture_one, alleles_one)
        step_mix = mixture_one - mixture
        curve_mix = mixture_two - mixture_one - step_mix
        step_allele = alleles_one - alleles
        curve_allele = alleles_two - alleles_one - step_allele
        alpha_mix = step_size(jnp.sum(step_mix * step_mix), jnp.sum(curve_mix * curve_mix))
        alpha_allele = step_size(jnp.sum(step_allele * step_allele), jnp.sum(curve_allele * curve_allele))
        extra_mix = tidy_mixture(mixture + 2.0 * alpha_mix * step_mix + alpha_mix * alpha_mix * curve_mix)
        extra_allele = clip_unit(alleles + 2.0 * alpha_allele * step_allele + alpha_allele * alpha_allele * curve_allele)
        mixture, alleles = expectation_step(genotypes, observed, twice_observed, extra_mix, extra_allele)
    return (mixture, alleles)
```

```python
import jax
import jax.numpy as jnp
from jax import lax
from jax.sharding import PartitionSpec as P

STEPS = 2


CLIP_LOW = 1e-05
NORM_EPS = 1e-10
EXACT = lax.Precision.HIGHEST


def clip_unit(values):
    return jnp.clip(values, CLIP_LOW, 1.0 - CLIP_LOW)


def tidy_mixture(mixture):
    clipped = clip_unit(mixture)
    return clipped / jnp.sum(clipped, axis=0, keepdims=True)


def step_size(first, second):
    return jnp.maximum(1.0, jnp.sqrt(first / (second + NORM_EPS)))


def allele_rule(alleles, alt_sums, ref_sums):
    weighted = alleles * alt_sums
    return clip_unit(weighted / (weighted + (1.0 - alleles) * ref_sums))


def exchange_sums(axis, first_radix):
    size = lax.axis_size(axis)
    rounds = []
    stride = 1
    while stride < size:
        left = size // stride
        radix = first_radix if stride == 1 and left % first_radix == 0 else 4
        while left % radix:
            radix //= 2
        if radix < 2:
            return lambda value: lax.psum(value, axis)
        rounds.append((stride, radix))
        stride *= radix

    def swap(value, mask):
        return lax.ppermute(value, axis, [(i, i ^ mask) for i in range(size)])

    def total(value):
        for stride, radix in rounds:
            parts = [value] + [swap(value, stride * m) for m in range(1, radix)]
            while len(parts) > 1:
                parts = [a + b for a, b in zip(parts[::2], parts[1::2])]
            value = parts[0]
        return value

    return total


def local(genotypes, observed, proportions, frequencies):
    samp_count = lax.axis_size("samp")
    var_count = lax.axis_size("var")
    populations = frequencies.shape[0]
    block_width = frequencies.shape[1]
    by_sample = lax.all_gather(frequencies, "samp", axis=1, tiled=True)
    by_sample = by_sample.reshape(populations, var_count, samp_count // var_count, block_width)
    arrived = lax.all_to_all(by_sample, "var", split_axis=1, concat_axis=1, tiled=True)
    alleles = jnp.transpose(arrived, (0, 2, 1, 3)).reshape(populations, -1)
    seen_vals = observed.astype(jnp.float32)
    geno_vals = genotypes.astype(jnp.float32)
    alt_counts = seen_vals * geno_vals
    ref_counts = seen_vals * (2.0 - geno_vals)
    local_counts = jnp.sum(observed, axis=1).astype(jnp.float32)[None, :]
    over_samp = exchange_sums("samp", 2)
    over_var = exchange_sums("var", 4)

    def expectation_sums(mixture, current):
        expected = lax.dot_general(
            mixture,
            current,
            (((0,), (0,)), ((), ())),
            precision=EXACT,
            preferred_element_type=jnp.float32,
        )
        ratio_alt = alt_counts / expected
        ratio_ref = ref_counts / (1.0 - expected)
        prop_terms = lax.dot_general(
            current,
            ratio_alt - ratio_ref,
            (((1,), (1,)), ((), ())),
            precision=EXACT,
            preferred_element_type=jnp.float32,
        )
        prop_terms = prop_terms + jnp.sum(ratio_ref, axis=1)[None, :]
        alt_terms = lax.dot_general(
            mixture,
            ratio_alt,
            (((1,), (0,)), ((), ())),
            precision=EXACT,
            preferred_element_type=jnp.float32,
        )
        ref_terms = lax.dot_general(
            mixture,
            ratio_ref,
            (((1,), (0,)), ((), ())),
            precision=EXACT,
            preferred_element_type=jnp.float32,
        )
        both_sums = over_samp(jnp.concatenate([alt_terms, ref_terms], axis=0))
        return prop_terms, both_sums

    def update(mixture, current, twice_observed, prop_sums, both_sums):
        next_mixture = clip_unit(mixture * prop_sums / twice_observed)
        next_alleles = allele_rule(current, both_sums[:populations], both_sums[populations:])
        return (next_mixture, next_alleles)

    mixture = proportions
    twice_observed = None
    for repeat in range(STEPS):
        prop_terms, both_sums = expectation_sums(mixture, alleles)
        if twice_observed is None:
            joined = over_var(jnp.concatenate([prop_terms, local_counts], axis=0))
            prop_sums = joined[:populations]
            twice_observed = 2.0 * joined[populations:]
        else:
            prop_sums = over_var(prop_terms)
        mixture_one, alleles_one = update(mixture, alleles, twice_observed, prop_sums, both_sums)
        prop_terms, both_sums = expectation_sums(mixture_one, alleles_one)
        mixture_two, alleles_two = update(
            mixture_one, alleles_one, twice_observed, over_var(prop_terms), both_sums
        )
        step_mix = mixture_one - mixture
        curve_mix = mixture_two - mixture_one - step_mix
        step_allele = alleles_one - alleles
        curve_allele = alleles_two - alleles_one - step_allele
        allele_squares = over_var(
            jnp.stack([jnp.sum(step_allele * step_allele), jnp.sum(curve_allele * curve_allele)])
        )
        mix_squares = over_samp(
            jnp.stack([jnp.sum(step_mix * step_mix), jnp.sum(curve_mix * curve_mix)])
        )
        alpha_mix = step_size(mix_squares[0], mix_squares[1])
        alpha_allele = step_size(allele_squares[0], allele_squares[1])
        extra_mix = tidy_mixture(
            mixture + 2.0 * alpha_mix * step_mix + alpha_mix * alpha_mix * curve_mix
        )
        extra_allele = clip_unit(
            alleles + 2.0 * alpha_allele * step_allele + alpha_allele * alpha_allele * curve_allele
        )
        prop_terms, both_sums = expectation_sums(extra_mix, extra_allele)
        mixture, alleles = update(
            extra_mix, extra_allele, twice_observed, over_var(prop_terms), both_sums
        )
    return (mixture, alleles)


def solution(mesh):
    placed = (P("samp", "var"), P("samp", "var"), P(None, "samp"), P(None, ("samp", "var")))
    return jax.shard_map(
        local,
        mesh=mesh,
        in_specs=placed,
        out_specs=(P(None, "samp"), P(None, "var")),
        check_vma=False,
    )
```

```python
import functools

import jax
import jax.numpy as jnp
from jax import lax
from jax.experimental import pallas as pl
from jax.experimental.pallas import tpu as pltpu
from jax.sharding import PartitionSpec as P

STEPS = 2
CLIP_LOW = 1e-05
NORM_EPS = 1e-10
F32 = jnp.float32
BF16 = jnp.bfloat16
SUBLANES = 8
LANES = 128
VMEM_BYTES = 40 * 2**20


def clip_unit(values):
    return jnp.clip(values, CLIP_LOW, 1.0 - CLIP_LOW)


def blocks_of(size, largest):
    width = min(size, largest)
    while size % width:
        width -= 1
    return width


def swap(value, axis, mask):
    size = lax.axis_size(axis)
    return lax.ppermute(value, axis, [(i, i ^ mask) for i in range(size)])


def partners(value, axis, stride, radix):
    return [value] + [swap(value, axis, stride * m) for m in range(1, radix)]


def pair_sum(parts):
    while len(parts) > 1:
        parts = [a + b for a, b in zip(parts[::2], parts[1::2])]
    return parts[0]


def rounds_of(size, first):
    rounds, stride = [], 1
    while stride < size:
        radix = first if stride == 1 else min(4, size // stride)
        rounds.append((stride, radix))
        stride *= radix
    return rounds


def last_parts(value, axis, first):
    rounds = rounds_of(lax.axis_size(axis), first)
    for stride, radix in rounds[:-1]:
        value = pair_sum(partners(value, axis, stride, radix))
    return partners(value, axis, *rounds[-1])


def gather_frequencies(frequencies):
    samp_count, var_count = lax.axis_size("samp"), lax.axis_size("var")
    group = samp_count // var_count
    samp, var = lax.axis_index("samp"), lax.axis_index("var")
    owner = samp // group
    both = ("samp", "var")
    arrived = [jnp.where(owner == var, frequencies, 0.0)]
    for mask in range(1, var_count):
        pairs = [
            (s * var_count + ((s // group) ^ mask), s * var_count + s // group)
            for s in range(samp_count)
        ]
        arrived.append(lax.ppermute(frequencies, both, pairs))
    stride = 1
    while stride < var_count:
        flip = (var & stride) != 0
        arrived = [jnp.where(flip, arrived[i ^ stride], arrived[i]) for i in range(var_count)]
        stride *= 2
    held = jnp.concatenate(arrived, axis=1)
    stride = 1
    while stride < group:
        other = swap(held, "samp", stride)
        upper = (samp & stride) != 0
        held = jnp.concatenate(
            [jnp.where(upper, other, held), jnp.where(upper, held, other)], axis=1
        )
        stride *= 2
    held = jnp.where(owner == var, held, 0.0)
    parts = [held]
    for mask in range(1, var_count):
        pairs = [
            ((v * group + g) * var_count + v, ((v ^ mask) * group + g) * var_count + v)
            for v in range(var_count)
            for g in range(group)
        ]
        parts.append(lax.ppermute(held, both, pairs))
    return pair_sum(parts)


def dot(left, right, left_dim, right_dim):
    return lax.dot_general(
        left, right, (((left_dim,), (right_dim,)), ((), ())), preferred_element_type=F32
    )


def split(values):
    high = values.astype(BF16)
    rest = values - high.astype(F32)
    middle = rest.astype(BF16)
    return high, middle, (rest - middle.astype(F32)).astype(BF16)


def ratio(counts, denominator):
    rounded = pl.reciprocal(denominator, approx=True).astype(BF16)
    error = 1.0 - denominator * rounded.astype(F32)
    high = counts * rounded
    return high, high * (error + error * error).astype(BF16)


def row_mask(values, populations):
    rows = lax.broadcasted_iota(jnp.int32, values.shape, 0)
    return jnp.where(rows < populations, values, 0.0)


def pad_rows(values, rows):
    spare = jnp.zeros((rows - values.shape[0], values.shape[1]), values.dtype)
    return jnp.concatenate([values, spare], axis=0)


def expectation(populations, mixture, alleles, alt_ref, ref_ref, prop_ref, both_ref, turned):
    rows, samples = mixture.shape
    variants = alleles.shape[1]
    tall, wide = blocks_of(samples, 256), blocks_of(variants, 512)
    mix_high, mix_mid, mix_low = split(mixture)
    all_high, all_mid, all_low = split(alleles)
    away = split(row_mask(1.0 - alleles, populations))
    turned[...] = jnp.concatenate(
        [mix_high, mix_high, mix_mid, mix_mid, mix_high, mix_low], axis=0
    ).T
    right = jnp.concatenate([all_high, all_mid, all_high, all_mid, all_low, all_high], axis=0)
    toward_turned = jnp.concatenate([all_high, all_mid, all_low], axis=0).T
    away_turned = jnp.concatenate(away, axis=0).T
    left = jnp.concatenate([mix_high, mix_mid, mix_low], axis=0)
    column_starts = range(0, variants, wide)
    alt_total = [jnp.zeros((3 * rows, wide), F32) for _ in column_starts]
    ref_total = [jnp.zeros((3 * rows, wide), F32) for _ in column_starts]
    for top in range(0, samples, tall):
        here = slice(top, top + tall)
        prop = jnp.zeros((tall, 3 * rows), F32)
        for index, start in enumerate(column_starts):
            across = slice(start, start + wide)
            expected = dot(turned[here, :], right[:, across], 1, 0)
            alt_high, alt_low = ratio(alt_ref[here, across], expected)
            ref_high, ref_low = ratio(ref_ref[here, across], 1.0 - expected)
            prop = (
                prop
                + dot(alt_high, toward_turned[across], 1, 0)
                + dot(alt_low, toward_turned[across], 1, 0)
                + dot(ref_high, away_turned[across], 1, 0)
                + dot(ref_low, away_turned[across], 1, 0)
            )
            weights = left[:, here]
            alt_total[index] = (
                alt_total[index] + dot(weights, alt_high, 1, 0) + dot(weights, alt_low, 1, 0)
            )
            ref_total[index] = (
                ref_total[index] + dot(weights, ref_high, 1, 0) + dot(weights, ref_low, 1, 0)
            )
        prop = prop.T
        prop_ref[:, here] = prop[:rows] + prop[rows : 2 * rows] + prop[2 * rows :]
    for index, start in enumerate(column_starts):
        across = slice(start, start + wide)
        alt, ref = alt_total[index], ref_total[index]
        alt = alt[:populations] + alt[rows : rows + populations] + alt[2 * rows : 2 * rows + populations]
        ref = ref[:populations] + ref[rows : rows + populations] + ref[2 * rows : 2 * rows + populations]
        both_ref[:, across] = jnp.concatenate([alt, ref], axis=0)


def update(populations, mixture, alleles, twice_observed, prop_parts, both_parts):
    prop_sums = pair_sum([part[...] for part in prop_parts])
    if twice_observed is None:
        twice_observed = prop_sums[populations : populations + 1]
    both_sums = pair_sum([part[...] for part in both_parts])
    rows = mixture.shape[0]
    next_mixture = row_mask(clip_unit(mixture * prop_sums / twice_observed), populations)
    alt_sums = both_sums[:populations]
    ref_sums = both_sums[populations : 2 * populations]
    current = alleles[:populations]
    weighted = current * alt_sums
    next_alleles = clip_unit(weighted / (weighted + (1.0 - current) * ref_sums))
    return next_mixture, pad_rows(next_alleles, rows), twice_observed


def prepare_kernel(genotypes, observed, alt_out, ref_out, count_out):
    samples = genotypes.shape[0]
    tall = blocks_of(samples, 128)
    ones = jnp.ones((SUBLANES, genotypes.shape[1]), BF16)
    for top in range(0, samples, tall):
        here = slice(top, top + tall)
        seen = observed[here, :]
        alt = seen * genotypes[here, :]
        alt_out[here, :] = alt.astype(F32).astype(BF16)
        ref_out[here, :] = (2 * seen - alt).astype(F32).astype(BF16)
        count_out[:, here] = 2.0 * dot(ones, seen.astype(F32).astype(BF16), 1, 1)


def first_kernel(
    mixture, alleles, counts, alt, ref, mixture_out, alleles_out, prop_out, both_out, turned
):
    populations = mixture.shape[0]
    rows = mixture_out.shape[0]
    mix = pad_rows(mixture[...], rows)
    current = pad_rows(alleles[...], rows)
    mixture_out[...] = mix
    alleles_out[...] = current
    expectation(populations, mix, current, alt, ref, prop_out, both_out, turned)
    prop_out[populations : populations + 1, :] = counts[:1, :]


def step_kernel(populations, n_prop, n_both, with_twice, *refs):
    refs = list(refs)
    mixture, alleles = refs[:2]
    twice = refs[2][...] if with_twice else None
    refs = refs[2 + with_twice :]
    prop_parts, both_parts = refs[:n_prop], refs[n_prop : n_prop + n_both]
    alt, ref = refs[n_prop + n_both : n_prop + n_both + 2]
    outs = refs[n_prop + n_both + 2 :]
    mix, current, twice = update(
        populations, mixture[...], alleles[...], twice, prop_parts, both_parts
    )
    outs[0][...] = mix
    outs[1][...] = current
    if not with_twice:
        outs[4][...] = twice
    expectation(populations, mix, current, alt, ref, outs[2], outs[3], outs[-1])


def folded(values):
    squares = values * values
    tile = squares.reshape(-1, SUBLANES, squares.shape[1]).sum(axis=0)
    width = tile.shape[1]
    return pair_sum_any([tile[:, i : i + LANES] for i in range(0, width, LANES)])


def pair_sum_any(parts):
    while len(parts) > 1:
        odd = parts[len(parts) // 2 * 2 :]
        parts = [a + b for a, b in zip(parts[::2], parts[1::2])] + odd
    return parts[0]


def square_kernel(populations, n_prop, n_both, *refs):
    mix_zero, all_zero, mix_one, all_one, twice = refs[:5]
    prop_parts, both_parts = refs[5 : 5 + n_prop], refs[5 + n_prop : 5 + n_prop + n_both]
    mix_out, all_out, mix_tile, all_tile = refs[5 + n_prop + n_both :]
    mix_two, all_two, _ = update(
        populations, mix_one[...], all_one[...], twice[...], prop_parts, both_parts
    )
    mix_out[...] = mix_two
    all_out[...] = all_two
    for zero, one, two, tile in (
        (mix_zero[...], mix_one[...], mix_two, mix_tile),
        (all_zero[...], all_one[...], all_two, all_tile),
    ):
        step = one - zero
        tile[:SUBLANES, :] = folded(step)
        tile[SUBLANES:, :] = folded(two - one - step)


def leap(zero, one, two, tile):
    first = jnp.sum(tile[:SUBLANES], axis=(0, 1), keepdims=True)
    second = jnp.sum(tile[SUBLANES:], axis=(0, 1), keepdims=True)
    alpha = jnp.maximum(1.0, jnp.sqrt(first / (second + NORM_EPS)))
    step = one - zero
    curve = two - one - step
    return zero + 2.0 * alpha * step + alpha * alpha * curve


def leap_kernel(populations, n_mix, n_all, *refs):
    states = [ref[...] for ref in refs[:6]]
    mix_zero, all_zero, mix_one, all_one, mix_two, all_two = states
    mix_parts, all_parts = refs[6 : 6 + n_mix], refs[6 + n_mix : 6 + n_mix + n_all]
    alt, ref, mixture_out, alleles_out, prop_out, both_out, turned = refs[6 + n_mix + n_all :]
    mix_tile = pair_sum([part[...] for part in mix_parts])
    all_tile = pair_sum([part[...] for part in all_parts])
    clipped = row_mask(clip_unit(leap(mix_zero, mix_one, mix_two, mix_tile)), populations)
    mix = clipped / jnp.sum(clipped, axis=0, keepdims=True)
    current = row_mask(clip_unit(leap(all_zero, all_one, all_two, all_tile)), populations)
    mixture_out[...] = mix
    alleles_out[...] = current
    expectation(populations, mix, current, alt, ref, prop_out, both_out, turned)


def final_kernel(populations, n_prop, n_both, mixture, alleles, twice, *refs):
    prop_parts, both_parts = refs[:n_prop], refs[n_prop : n_prop + n_both]
    mixture_out, alleles_out = refs[n_prop + n_both :]
    mix, current, _ = update(
        populations, mixture[...], alleles[...], twice[...], prop_parts, both_parts
    )
    mixture_out[...] = mix[:populations]
    alleles_out[...] = current[:populations]


def call(kernel, name, outs, args, scratch=()):
    whole = pl.BlockSpec(memory_space=pltpu.VMEM)
    return pl.pallas_call(
        kernel,
        out_shape=tuple(jax.ShapeDtypeStruct(*out) for out in outs),
        in_specs=[whole] * len(args),
        out_specs=(whole,) * len(outs),
        scratch_shapes=list(scratch),
        compiler_params=pltpu.CompilerParams(vmem_limit_bytes=VMEM_BYTES),
        name=name,
    )(*args)


def local(genotypes, observed, proportions, frequencies):
    populations, samples = proportions.shape
    variants = genotypes.shape[1]
    rows = -(-(populations + 1) // 16) * 16
    mix_out, all_out = ((rows, samples), F32), ((rows, variants), F32)
    both_out = ((2 * populations, variants), F32)
    tile_out = ((2 * SUBLANES, LANES), F32)
    turned = (pltpu.VMEM((samples, 6 * rows), BF16),)
    tables = [((samples, variants), BF16)] * 2

    alleles = gather_frequencies(frequencies)
    alt, ref, counts = call(
        prepare_kernel, "prepare", tables + [((SUBLANES, samples), F32)], (genotypes, observed)
    )

    def exchanged(prop, both):
        return last_parts(prop, "var", 4), last_parts(both, "samp", 2)

    mix_zero, all_zero, prop, both = call(
        first_kernel,
        "first",
        (mix_out, all_out, mix_out, both_out),
        (proportions, alleles, counts, alt, ref),
        turned,
    )
    twice = None
    for repeat in range(STEPS):
        if repeat:
            prop_parts, both_parts = exchanged(prop, both)
            mix_zero, all_zero, prop, both = call(
                functools.partial(
                    step_kernel, populations, len(prop_parts), len(both_parts), 1
                ),
                "step",
                (mix_out, all_out, mix_out, both_out),
                (mix_zero, all_zero, twice, *prop_parts, *both_parts, alt, ref),
                turned,
            )
        prop_parts, both_parts = exchanged(prop, both)
        known = () if twice is None else (twice,)
        extra = () if known else (((1, samples), F32),)
        mix_one, all_one, prop, both, *found = call(
            functools.partial(
                step_kernel, populations, len(prop_parts), len(both_parts), len(known)
            ),
            "step",
            (mix_out, all_out, mix_out, both_out, *extra),
            (mix_zero, all_zero, *known, *prop_parts, *both_parts, alt, ref),
            turned,
        )
        (twice,) = known or found
        prop_parts, both_parts = exchanged(prop, both)
        mix_two, all_two, mix_tile, all_tile = call(
            functools.partial(square_kernel, populations, len(prop_parts), len(both_parts)),
            "square",
            (mix_out, all_out, tile_out, tile_out),
            (mix_zero, all_zero, mix_one, all_one, twice, *prop_parts, *both_parts),
        )
        mix_parts = last_parts(mix_tile, "samp", 2)
        all_parts = last_parts(all_tile, "var", 4)
        mix_zero, all_zero, prop, both = call(
            functools.partial(leap_kernel, populations, len(mix_parts), len(all_parts)),
            "leap",
            (mix_out, all_out, mix_out, both_out),
            (mix_zero, all_zero, mix_one, all_one, mix_two, all_two, *mix_parts, *all_parts, alt, ref),
            turned,
        )
    prop_parts, both_parts = exchanged(prop, both)
    return call(
        functools.partial(final_kernel, populations, len(prop_parts), len(both_parts)),
        "final",
        (((populations, samples), F32), ((populations, variants), F32)),
        (mix_zero, all_zero, twice, *prop_parts, *both_parts),
    )


def solution(mesh):
    placed = (P("samp", "var"), P("samp", "var"), P(None, "samp"), P(None, ("samp", "var")))
    return jax.shard_map(
        local,
        mesh=mesh,
        in_specs=placed,
        out_specs=(P(None, "samp"), P(None, "var")),
        check_vma=False,
    )
```

```python
import functools

import jax
import jax.numpy as jnp
from jax import lax
from jax.experimental import pallas as pl
from jax.experimental.pallas import tpu as pltpu
from jax.sharding import PartitionSpec as P

STEPS = 2
CLIP_LOW = 1e-05
NORM_EPS = 1e-10
F32 = jnp.float32
BF16 = jnp.bfloat16
SUBLANES = 8
LANES = 128
VMEM_BYTES = 40 * 2**20


def clip_unit(values):
    return jnp.clip(values, CLIP_LOW, 1.0 - CLIP_LOW)


def blocks_of(size, largest):
    width = min(size, largest)
    while size % width:
        width -= 1
    return width


def swap(value, axis, mask):
    size = lax.axis_size(axis)
    return lax.ppermute(value, axis, [(i, i ^ mask) for i in range(size)])


def last_parts(value, axis):
    size, stride = lax.axis_size(axis), 1
    while 2 * stride < size:
        value = value + swap(value, axis, stride)
        stride *= 2
    return value, swap(value, axis, stride)


def gather_frequencies(frequencies):
    samp_count, var_count = lax.axis_size("samp"), lax.axis_size("var")
    group = samp_count // var_count
    samp, var = lax.axis_index("samp"), lax.axis_index("var")
    owner = samp // group
    both = ("samp", "var")
    arrived = [jnp.where(owner == var, frequencies, 0.0)]
    for mask in range(1, var_count):
        pairs = [
            (s * var_count + ((s // group) ^ mask), s * var_count + s // group)
            for s in range(samp_count)
        ]
        arrived.append(lax.ppermute(frequencies, both, pairs))
    stride = 1
    while stride < var_count:
        flip = (var & stride) != 0
        arrived = [jnp.where(flip, arrived[i ^ stride], arrived[i]) for i in range(var_count)]
        stride *= 2
    held = jnp.concatenate(arrived, axis=1)
    stride = 1
    while stride < group:
        other = swap(held, "samp", stride)
        upper = (samp & stride) != 0
        held = jnp.concatenate(
            [jnp.where(upper, other, held), jnp.where(upper, held, other)], axis=1
        )
        stride *= 2
    held = jnp.where(owner == var, held, 0.0)
    total = held
    for mask in range(1, var_count):
        pairs = [
            ((v * group + g) * var_count + v, ((v ^ mask) * group + g) * var_count + v)
            for v in range(var_count)
            for g in range(group)
        ]
        total = total + lax.ppermute(held, both, pairs)
    return total


def dot(left, right, left_dim, right_dim):
    return lax.dot_general(
        left, right, (((left_dim,), (right_dim,)), ((), ())), preferred_element_type=F32
    )


def split(values):
    high = values.astype(BF16)
    rest = values - high.astype(F32)
    middle = rest.astype(BF16)
    return high, middle, (rest - middle.astype(F32)).astype(BF16)


def ratio(counts, denominator):
    inverse = pl.reciprocal(denominator, approx=True)
    high = inverse.astype(BF16)
    low = (inverse - high.astype(F32)).astype(BF16)
    return counts * high, counts * low


def row_mask(values, populations):
    rows = lax.broadcasted_iota(jnp.int32, values.shape, 0)
    return jnp.where(rows < populations, values, 0.0)


def pad_rows(values, rows):
    spare = jnp.zeros((rows - values.shape[0], values.shape[1]), values.dtype)
    return jnp.concatenate([values, spare], axis=0)


def put_packed(ref, first, stride, values):
    count = values.shape[0]
    for block in range(values.shape[1] // LANES):
        top = block * stride + first
        ref[top : top + count, :] = values[:, block * LANES : (block + 1) * LANES]


def sum_packed(parts, first, stride, count):
    one, other = parts
    pieces = []
    for top in range(first, one.shape[0], stride):
        here = slice(top, top + count)
        pieces.append(one[here, :] + other[here, :])
    return jnp.concatenate(pieces, axis=1)


def expectation(populations, mixture, alleles, alt_ref, ref_ref, prop_ref, both_ref, turned, counts=None):
    rows, samples = mixture.shape
    variants = alleles.shape[1]
    tall, wide = blocks_of(samples, 1024), blocks_of(variants, 512)
    mix_high, mix_mid, mix_low = split(mixture)
    all_high, all_mid, all_low = split(alleles)
    away_high, away_mid, _ = split(row_mask(1.0 - alleles, populations))
    turned[...] = jnp.concatenate(
        [mix_high, mix_high, mix_mid, mix_mid, mix_high, mix_low], axis=0
    ).T
    right = jnp.concatenate([all_high, all_mid, all_high, all_mid, all_low, all_high], axis=0)
    toward = jnp.concatenate([all_high, all_mid], axis=0)
    away = jnp.concatenate([away_high, away_mid], axis=0)
    left = jnp.concatenate([mix_high, mix_mid], axis=0)
    column_starts = range(0, variants, wide)
    alt_total = [jnp.zeros((2 * rows, wide), F32) for _ in column_starts]
    ref_total = [jnp.zeros((2 * rows, wide), F32) for _ in column_starts]
    props = []
    for top in range(0, samples, tall):
        here = slice(top, top + tall)
        prop = jnp.zeros((2 * rows, tall), F32)
        for index, start in enumerate(column_starts):
            across = slice(start, start + wide)
            expected = dot(turned[here, :], right[:, across], 1, 0)
            alt_high, alt_low = ratio(alt_ref[here, across], expected)
            ref_high, ref_low = ratio(ref_ref[here, across], 1.0 - expected)
            prop = (
                prop
                + dot(toward[:, across], alt_high, 1, 1)
                + dot(toward[:, across], alt_low, 1, 1)
                + dot(away[:, across], ref_high, 1, 1)
                + dot(away[:, across], ref_low, 1, 1)
            )
            weights = left[:, here]
            alt_total[index] = (
                alt_total[index] + dot(weights, alt_high, 1, 0) + dot(weights, alt_low, 1, 0)
            )
            ref_total[index] = (
                ref_total[index] + dot(weights, ref_high, 1, 0) + dot(weights, ref_low, 1, 0)
            )
        props.append(prop[:populations] + prop[rows : rows + populations])
    stride = prop_ref.shape[0] * LANES // samples
    put_packed(prop_ref, 0, stride, jnp.concatenate(props, axis=1))
    if counts is not None:
        put_packed(prop_ref, populations, stride, counts)
    for place, totals in enumerate((alt_total, ref_total)):
        sums = jnp.concatenate(totals, axis=1)
        sums = sums[:populations] + sums[rows : rows + populations]
        put_packed(both_ref, place * populations, 2 * populations, sums)


def update(populations, mixture, alleles, twice_observed, prop_parts, both_parts):
    rows, samples = mixture.shape
    stride = prop_parts[0].shape[0] * LANES // samples
    prop_sums = sum_packed(prop_parts, 0, stride, populations)
    if twice_observed is None:
        twice_observed = sum_packed(prop_parts, populations, stride, 1)
    alt_sums = sum_packed(both_parts, 0, 2 * populations, populations)
    ref_sums = sum_packed(both_parts, populations, 2 * populations, populations)
    next_mixture = clip_unit(mixture[:populations] * prop_sums / twice_observed)
    current = alleles[:populations]
    weighted = current * alt_sums
    next_alleles = clip_unit(weighted / (weighted + (1.0 - current) * ref_sums))
    return pad_rows(next_mixture, rows), pad_rows(next_alleles, rows), twice_observed


def prepare_kernel(genotypes, observed, alt_out, ref_out, count_out, landed, arrivals):
    samples, variants = genotypes.shape
    tall = blocks_of(samples, 128)
    copies = []
    for index, top in enumerate(range(0, samples, tall)):
        here = pl.ds(top, tall)
        for place, source in enumerate((genotypes, observed)):
            copy = pltpu.make_async_copy(
                source.at[here, :], landed.at[place, here, :], arrivals.at[place, index]
            )
            copy.start()
            copies.append(copy)
    ones = jnp.ones((SUBLANES, variants), BF16)
    for index, top in enumerate(range(0, samples, tall)):
        here = slice(top, top + tall)
        copies[2 * index].wait()
        copies[2 * index + 1].wait()
        seen = landed[1, here, :]
        alt = seen * landed[0, here, :]
        alt_out[here, :] = alt.astype(F32).astype(BF16)
        ref_out[here, :] = (2 * seen - alt).astype(F32).astype(BF16)
        count_out[:, here] = 2.0 * dot(ones, seen.astype(F32).astype(BF16), 1, 1)


def first_kernel(
    mixture, alleles, counts, alt, ref, mixture_out, alleles_out, prop_out, both_out, turned
):
    populations = mixture.shape[0]
    rows = mixture_out.shape[0]
    mix = pad_rows(mixture[...], rows)
    current = pad_rows(alleles[...], rows)
    mixture_out[...] = mix
    alleles_out[...] = current
    expectation(
        populations, mix, current, alt, ref, prop_out, both_out, turned, counts[:1, :]
    )


def step_kernel(populations, with_twice, *refs):
    mixture, alleles = refs[:2]
    twice = refs[2][...] if with_twice else None
    prop_parts, both_parts, (alt, ref), outs = split_refs(refs[2 + with_twice :], 2, 2, 2)
    mix, current, twice = update(
        populations, mixture[...], alleles[...], twice, prop_parts, both_parts
    )
    outs[0][...] = mix
    outs[1][...] = current
    if not with_twice:
        outs[4][...] = twice
    expectation(populations, mix, current, alt, ref, outs[2], outs[3], outs[-1])


def split_refs(refs, *counts):
    groups = []
    for count in counts:
        groups.append(refs[:count])
        refs = refs[count:]
    return (*groups, refs)


def folded(values):
    squares = values * values
    tile = squares.reshape(-1, SUBLANES, squares.shape[1]).sum(axis=0)
    width = tile.shape[1]
    return sum(tile[:, i : i + LANES] for i in range(0, width, LANES))


def square_kernel(populations, *refs):
    mix_zero, all_zero, mix_one, all_one, twice = refs[:5]
    prop_parts, both_parts, (mix_out, all_out, mix_tile, all_tile) = split_refs(refs[5:], 2, 2)
    mix_two, all_two, _ = update(
        populations, mix_one[...], all_one[...], twice[...], prop_parts, both_parts
    )
    mix_out[...] = mix_two
    all_out[...] = all_two
    for zero, one, two, tile in (
        (mix_zero[...], mix_one[...], mix_two, mix_tile),
        (all_zero[...], all_one[...], all_two, all_tile),
    ):
        step = one - zero
        tile[:SUBLANES, :] = folded(step)
        tile[SUBLANES:, :] = folded(two - one - step)


def leap(zero, one, two, tile):
    first = jnp.sum(tile[:SUBLANES], axis=(0, 1), keepdims=True)
    second = jnp.sum(tile[SUBLANES:], axis=(0, 1), keepdims=True)
    alpha = jnp.maximum(1.0, jnp.sqrt(first / (second + NORM_EPS)))
    step = one - zero
    curve = two - one - step
    return zero + 2.0 * alpha * step + alpha * alpha * curve


def leap_kernel(populations, *refs):
    states = [ref[...] for ref in refs[:6]]
    mix_zero, all_zero, mix_one, all_one, mix_two, all_two = states
    mix_parts, all_parts, rest = split_refs(refs[6:], 2, 2)
    alt, ref, mixture_out, alleles_out, prop_out, both_out, turned = rest
    mix_tile = mix_parts[0][...] + mix_parts[1][...]
    all_tile = all_parts[0][...] + all_parts[1][...]
    clipped = row_mask(clip_unit(leap(mix_zero, mix_one, mix_two, mix_tile)), populations)
    mix = clipped / jnp.sum(clipped, axis=0, keepdims=True)
    current = row_mask(clip_unit(leap(all_zero, all_one, all_two, all_tile)), populations)
    mixture_out[...] = mix
    alleles_out[...] = current
    expectation(populations, mix, current, alt, ref, prop_out, both_out, turned)


def final_kernel(populations, mixture, alleles, twice, *refs):
    prop_parts, both_parts, (mixture_out, alleles_out) = split_refs(refs, 2, 2)
    mix, current, _ = update(
        populations, mixture[...], alleles[...], twice[...], prop_parts, both_parts
    )
    mixture_out[...] = mix[:populations]
    alleles_out[...] = current[:populations]


def call(kernel, name, outs, args, scratch=(), space=pltpu.VMEM):
    whole = pl.BlockSpec(memory_space=pltpu.VMEM)
    return pl.pallas_call(
        kernel,
        out_shape=tuple(jax.ShapeDtypeStruct(*out) for out in outs),
        in_specs=[pl.BlockSpec(memory_space=space)] * len(args),
        out_specs=(whole,) * len(outs),
        scratch_shapes=list(scratch),
        compiler_params=pltpu.CompilerParams(vmem_limit_bytes=VMEM_BYTES),
        name=name,
    )(*args)


def local(genotypes, observed, proportions, frequencies):
    populations, samples = proportions.shape
    variants = genotypes.shape[1]
    rows = -(-populations // 16) * 16
    state_out = (((rows, samples), F32), ((rows, variants), F32))
    packed = populations * samples // LANES
    both_out = ((2 * populations * variants // LANES, LANES), F32)
    sums_out = (((packed, LANES), F32), both_out)
    first_sums_out = (((packed + samples // LANES, LANES), F32), both_out)
    tile_out = ((2 * SUBLANES, LANES), F32)
    turned = (pltpu.VMEM((samples, 6 * rows), BF16),)
    table_out = ((samples, variants), BF16)
    chunks = samples // blocks_of(samples, 128)

    alleles = gather_frequencies(frequencies)
    alt, ref, counts = call(
        prepare_kernel,
        "prepare",
        (table_out, table_out, ((SUBLANES, samples), F32)),
        (genotypes, observed),
        (
            pltpu.VMEM((2, samples, variants), jnp.int32),
            pltpu.SemaphoreType.DMA((2, chunks)),
        ),
        pl.ANY,
    )

    def exchanged(prop, both):
        return (*last_parts(prop, "var"), *last_parts(both, "samp"))

    mix_zero, all_zero, prop, both = call(
        first_kernel,
        "first",
        (*state_out, *first_sums_out),
        (proportions, alleles, counts, alt, ref),
        turned,
    )
    twice = None
    for repeat in range(STEPS):
        if repeat:
            mix_zero, all_zero, prop, both = call(
                functools.partial(step_kernel, populations, 1),
                "step",
                (*state_out, *sums_out),
                (mix_zero, all_zero, twice, *exchanged(prop, both), alt, ref),
                turned,
            )
        known = () if twice is None else (twice,)
        extra = () if known else (((1, samples), F32),)
        mix_one, all_one, prop, both, *found = call(
            functools.partial(step_kernel, populations, len(known)),
            "step",
            (*state_out, *sums_out, *extra),
            (mix_zero, all_zero, *known, *exchanged(prop, both), alt, ref),
            turned,
        )
        (twice,) = known or found
        mix_two, all_two, mix_tile, all_tile = call(
            functools.partial(square_kernel, populations),
            "square",
            (*state_out, tile_out, tile_out),
            (mix_zero, all_zero, mix_one, all_one, twice, *exchanged(prop, both)),
        )
        tiles = (*last_parts(mix_tile, "samp"), *last_parts(all_tile, "var"))
        mix_zero, all_zero, prop, both = call(
            functools.partial(leap_kernel, populations),
            "leap",
            (*state_out, *sums_out),
            (mix_zero, all_zero, mix_one, all_one, mix_two, all_two, *tiles, alt, ref),
            turned,
        )
    return call(
        functools.partial(final_kernel, populations),
        "final",
        (((populations, samples), F32), ((populations, variants), F32)),
        (mix_zero, all_zero, twice, *exchanged(prop, both)),
    )


def solution(mesh):
    placed = (P("samp", "var"), P("samp", "var"), P(None, "samp"), P(None, ("samp", "var")))
    return jax.shard_map(
        local,
        mesh=mesh,
        in_specs=placed,
        out_specs=(P(None, "samp"), P(None, "var")),
        check_vma=False,
    )
```

```python
import functools

import jax
import jax.numpy as jnp
from jax import lax
from jax.experimental import pallas as pl
from jax.experimental.pallas import tpu as pltpu
from jax.sharding import PartitionSpec as P

STEPS = 2
CLIP_LOW = 1e-05
NORM_EPS = 1e-10
F32 = jnp.float32
BF16 = jnp.bfloat16
SUBLANES = 8
LANES = 128
VMEM_BYTES = 40 * 2**20
MIXTURE_COST = 5 * 10**9


def clip_unit(values):
    return jnp.clip(values, CLIP_LOW, 1.0 - CLIP_LOW)


def blocks_of(size, largest):
    width = min(size, largest)
    while size % width:
        width -= 1
    return width


def swap(value, axis, mask):
    size = lax.axis_size(axis)
    return lax.ppermute(value, axis, [(i, i ^ mask) for i in range(size)])


def strides_of(axis):
    return [1 << bit for bit in range(lax.axis_size(axis).bit_length() - 1)]


def all_parts_of(value, axis):
    return [value] + [swap(value, axis, mask) for mask in range(1, lax.axis_size(axis))]


def pair_sum(parts):
    while len(parts) > 1:
        parts = [a + b for a, b in zip(parts[::2], parts[1::2])]
    return parts[0]


def parts_of(value, axis):
    strides = strides_of(axis)
    for stride in strides[:-1]:
        value = value + swap(value, axis, stride)
    return value, swap(value, axis, strides[-1])


def gather_frequencies(frequencies):
    samp_count, var_count = lax.axis_size("samp"), lax.axis_size("var")
    group = samp_count // var_count
    samp, var = lax.axis_index("samp"), lax.axis_index("var")
    owner = samp // group
    both = ("samp", "var")
    arrived = [jnp.where(owner == var, frequencies, 0.0)]
    for mask in range(1, var_count):
        pairs = [
            (s * var_count + ((s // group) ^ mask), s * var_count + s // group)
            for s in range(samp_count)
        ]
        arrived.append(lax.ppermute(frequencies, both, pairs))
    stride = 1
    while stride < var_count:
        flip = (var & stride) != 0
        arrived = [jnp.where(flip, arrived[i ^ stride], arrived[i]) for i in range(var_count)]
        stride *= 2
    held = jnp.concatenate(arrived, axis=1)
    stride = 1
    while stride < group:
        other = swap(held, "samp", stride)
        upper = (samp & stride) != 0
        held = jnp.concatenate(
            [jnp.where(upper, other, held), jnp.where(upper, held, other)], axis=1
        )
        stride *= 2
    held = jnp.where(owner == var, held, 0.0)
    total = held
    for mask in range(1, var_count):
        pairs = [
            ((v * group + g) * var_count + v, ((v ^ mask) * group + g) * var_count + v)
            for v in range(var_count)
            for g in range(group)
        ]
        total = total + lax.ppermute(held, both, pairs)
    return total


def dot(left, right, left_dim, right_dim):
    return lax.dot_general(
        left, right, (((left_dim,), (right_dim,)), ((), ())), preferred_element_type=F32
    )


def split(values):
    high = values.astype(BF16)
    rest = values - high.astype(F32)
    middle = rest.astype(BF16)
    return high, middle, (rest - middle.astype(F32)).astype(BF16)


def ratio(counts, denominator):
    inverse = pl.reciprocal(denominator, approx=True)
    high = inverse.astype(BF16)
    low = (inverse - high.astype(F32)).astype(BF16)
    return counts * high, counts * low


def row_mask(values, populations):
    rows = lax.broadcasted_iota(jnp.int32, values.shape, 0)
    return jnp.where(rows < populations, values, 0.0)


def pad_rows(values, rows):
    spare = jnp.zeros((rows - values.shape[0], values.shape[1]), values.dtype)
    return jnp.concatenate([values, spare], axis=0)


def put_packed(ref, first, stride, values):
    count = values.shape[0]
    for block in range(values.shape[1] // LANES):
        top = block * stride + first
        ref[top : top + count, :] = values[:, block * LANES : (block + 1) * LANES]


def sum_packed(parts, first, stride, count):
    pieces = []
    for top in range(first, parts[0].shape[0], stride):
        here = slice(top, top + count)
        pieces.append(pair_sum([part[here, :] for part in parts]))
    return jnp.concatenate(pieces, axis=1)


def expectation(populations, mixture, alleles, alt_ref, ref_ref, prop_ref, both_ref, turned, counts=None):
    rows, samples = mixture.shape
    variants = alleles.shape[1]
    tall, wide = blocks_of(samples, 1024), blocks_of(variants, 512)
    mix_high, mix_mid, mix_low = split(mixture)
    all_high, all_mid, all_low = split(alleles)
    away_high, away_mid, _ = split(row_mask(1.0 - alleles, populations))
    turned[...] = jnp.concatenate(
        [mix_high, mix_high, mix_mid, mix_mid, mix_high, mix_low], axis=0
    ).T
    right = jnp.concatenate([all_high, all_mid, all_high, all_mid, all_low, all_high], axis=0)
    toward = jnp.concatenate([all_high, all_mid], axis=0)
    away = jnp.concatenate([away_high, away_mid], axis=0)
    left = jnp.concatenate([mix_high, mix_mid], axis=0)
    column_starts = range(0, variants, wide)
    alt_total = [jnp.zeros((2 * rows, wide), F32) for _ in column_starts]
    ref_total = [jnp.zeros((2 * rows, wide), F32) for _ in column_starts]
    props = []
    for top in range(0, samples, tall):
        here = slice(top, top + tall)
        prop = jnp.zeros((2 * rows, tall), F32)
        for index, start in enumerate(column_starts):
            across = slice(start, start + wide)
            expected = dot(turned[here, :], right[:, across], 1, 0)
            alt_high, alt_low = ratio(alt_ref[here, across], expected)
            ref_high, ref_low = ratio(ref_ref[here, across], 1.0 - expected)
            prop = (
                prop
                + dot(toward[:, across], alt_high, 1, 1)
                + dot(toward[:, across], alt_low, 1, 1)
                + dot(away[:, across], ref_high, 1, 1)
                + dot(away[:, across], ref_low, 1, 1)
            )
            weights = left[:, here]
            alt_total[index] = (
                alt_total[index] + dot(weights, alt_high, 1, 0) + dot(weights, alt_low, 1, 0)
            )
            ref_total[index] = (
                ref_total[index] + dot(weights, ref_high, 1, 0) + dot(weights, ref_low, 1, 0)
            )
        props.append(prop[:populations] + prop[rows : rows + populations])
    stride = prop_ref.shape[0] * LANES // samples
    put_packed(prop_ref, 0, stride, jnp.concatenate(props, axis=1))
    if counts is not None:
        put_packed(prop_ref, populations, stride, counts)
    for place, totals in enumerate((alt_total, ref_total)):
        sums = jnp.concatenate(totals, axis=1)
        sums = sums[:populations] + sums[rows : rows + populations]
        put_packed(both_ref, place * populations, 2 * populations, sums)


def next_mixture(populations, mixture, twice_observed, prop_parts):
    rows, samples = mixture.shape
    stride = prop_parts[0].shape[0] * LANES // samples
    prop_sums = sum_packed(prop_parts, 0, stride, populations)
    if twice_observed is None:
        twice_observed = sum_packed(prop_parts, populations, stride, 1)
    moved = clip_unit(mixture[:populations] * prop_sums / twice_observed)
    return pad_rows(moved, rows), twice_observed


def next_alleles(populations, alleles, both_parts):
    alt_sums = sum_packed(both_parts, 0, 2 * populations, populations)
    ref_sums = sum_packed(both_parts, populations, 2 * populations, populations)
    current = alleles[:populations]
    weighted = current * alt_sums
    moved = clip_unit(weighted / (weighted + (1.0 - current) * ref_sums))
    return pad_rows(moved, alleles.shape[0])


def first_kernel(mixture, alleles, alt, ref, mixture_out, alleles_out, prop_out, both_out, turned):
    populations = mixture.shape[0]
    rows = mixture_out.shape[0]
    mix = pad_rows(mixture[...], rows)
    current = pad_rows(alleles[...], rows)
    mixture_out[...] = mix
    alleles_out[...] = current
    ones = jnp.ones((SUBLANES, alt.shape[1]), BF16)
    twice_observed = dot(ones, alt[...], 1, 1) + dot(ones, ref[...], 1, 1)
    expectation(
        populations, mix, current, alt, ref, prop_out, both_out, turned, twice_observed[:1]
    )


def mixture_kernel(populations, with_twice, mixture, *refs):
    twice = refs[0][...] if with_twice else None
    prop_parts, outs = split_refs(refs[with_twice:], len(refs) - 2)
    mix, twice = next_mixture(populations, mixture[...], twice, prop_parts)
    outs[0][...] = mix
    if not with_twice:
        outs[1][...] = twice


def step_kernel(populations, mixture, alleles, *refs):
    both_parts, (alt, ref, alleles_out, prop_out, both_out, turned) = split_refs(refs, 2)
    current = next_alleles(populations, alleles[...], both_parts)
    alleles_out[...] = current
    expectation(populations, mixture[...], current, alt, ref, prop_out, both_out, turned)


def split_refs(refs, *counts):
    groups = []
    for count in counts:
        groups.append(refs[:count])
        refs = refs[count:]
    return (*groups, refs)


def folded(values):
    squares = values * values
    tile = squares.reshape(-1, SUBLANES, squares.shape[1]).sum(axis=0)
    width = tile.shape[1]
    return sum(tile[:, i : i + LANES] for i in range(0, width, LANES))


def squares(zero, one, two, tile):
    step = one - zero
    tile[:SUBLANES, :] = folded(step)
    tile[SUBLANES:, :] = folded(two - one - step)


def mixture_square_kernel(populations, zero, one, twice, *refs):
    prop_parts, (two_out, tile) = split_refs(refs, len(refs) - 2)
    two, _ = next_mixture(populations, one[...], twice[...], prop_parts)
    two_out[...] = two
    squares(zero[...], one[...], two, tile)


def alleles_square_kernel(populations, zero, one, *refs):
    both_parts, (two_out, tile) = split_refs(refs, 2)
    two = next_alleles(populations, one[...], both_parts)
    two_out[...] = two
    squares(zero[...], one[...], two, tile)


def leap(zero, one, two, tile):
    first = jnp.sum(tile[:SUBLANES], axis=(0, 1), keepdims=True)
    second = jnp.sum(tile[SUBLANES:], axis=(0, 1), keepdims=True)
    alpha = jnp.maximum(1.0, jnp.sqrt(first / (second + NORM_EPS)))
    step = one - zero
    curve = two - one - step
    return zero + 2.0 * alpha * step + alpha * alpha * curve


def leap_kernel(populations, *refs):
    states = [ref[...] for ref in refs[:6]]
    mix_zero, all_zero, mix_one, all_one, mix_two, all_two = states
    mix_parts, all_parts, rest = split_refs(refs[6:], 2, 2)
    alt, ref, mixture_out, alleles_out, prop_out, both_out, turned = rest
    mix_tile = mix_parts[0][...] + mix_parts[1][...]
    all_tile = all_parts[0][...] + all_parts[1][...]
    clipped = row_mask(clip_unit(leap(mix_zero, mix_one, mix_two, mix_tile)), populations)
    mix = clipped / jnp.sum(clipped, axis=0, keepdims=True)
    current = row_mask(clip_unit(leap(all_zero, all_one, all_two, all_tile)), populations)
    mixture_out[...] = mix
    alleles_out[...] = current
    expectation(populations, mix, current, alt, ref, prop_out, both_out, turned)


def last_mixture_kernel(populations, mixture, twice, *refs):
    prop_parts, (out,) = split_refs(refs, len(refs) - 1)
    mix, _ = next_mixture(populations, mixture[...], twice[...], prop_parts)
    out[...] = mix[:populations]


def last_alleles_kernel(populations, alleles, *refs):
    both_parts, (out,) = split_refs(refs, 2)
    out[...] = next_alleles(populations, alleles[...], both_parts)[:populations]


def call(kernel, name, outs, args, scratch=(), moved=0):
    whole = pl.BlockSpec(memory_space=pltpu.VMEM)
    cost = pl.CostEstimate(flops=moved, bytes_accessed=0, transcendentals=0) if moved else None
    return pl.pallas_call(
        kernel,
        out_shape=tuple(jax.ShapeDtypeStruct(*out) for out in outs),
        in_specs=[pl.BlockSpec(memory_space=pltpu.VMEM)] * len(args),
        out_specs=(whole,) * len(outs),
        scratch_shapes=list(scratch),
        compiler_params=pltpu.CompilerParams(vmem_limit_bytes=VMEM_BYTES),
        cost_estimate=cost,
        name=name,
    )(*args)


def local(genotypes, observed, proportions, frequencies):
    populations, samples = proportions.shape
    variants = genotypes.shape[1]
    rows = -(-populations // 16) * 16
    state_out = (((rows, samples), F32), ((rows, variants), F32))
    packed = populations * samples // LANES
    both_out = ((2 * populations * variants // LANES, LANES), F32)
    sums_out = (((packed, LANES), F32), both_out)
    first_sums_out = (((packed + samples // LANES, LANES), F32), both_out)
    tile_out = ((2 * SUBLANES, LANES), F32)
    turned = (pltpu.VMEM((samples, 6 * rows), BF16),)

    alleles = gather_frequencies(frequencies)
    alt = (observed * genotypes).astype(BF16)
    ref = (observed * (2 - genotypes)).astype(BF16)

    mix_zero, all_zero, prop, both = call(
        first_kernel,
        "first",
        (*state_out, *first_sums_out),
        (proportions, alleles, alt, ref),
        turned,
    )

    def moved_mixture(mixture, twice, prop):
        known = () if twice is None else (twice,)
        extra = () if known else (((1, samples), F32),)
        out = call(
            functools.partial(mixture_kernel, populations, len(known)),
            "mixture",
            (state_out[0], *extra),
            (mixture, *known, *all_parts_of(prop, "var")),
            moved=MIXTURE_COST,
        )
        return out[0], (known or out[1:])[0]

    def step(mixture, alleles, both):
        return call(
            functools.partial(step_kernel, populations),
            "step",
            (state_out[1], *sums_out),
            (mixture, alleles, *parts_of(both, "samp"), alt, ref),
            turned,
        )

    twice = None
    for repeat in range(STEPS):
        if repeat:
            mix_zero, twice = moved_mixture(mix_zero, twice, prop)
            all_zero, prop, both = step(mix_zero, all_zero, both)
        mix_one, twice = moved_mixture(mix_zero, twice, prop)
        all_one, prop, both = step(mix_one, all_zero, both)
        mix_two, mix_tile = call(
            functools.partial(mixture_square_kernel, populations),
            "mixture_square",
            (state_out[0], tile_out),
            (mix_zero, mix_one, twice, *all_parts_of(prop, "var")),
            moved=MIXTURE_COST,
        )
        all_two, all_tile = call(
            functools.partial(alleles_square_kernel, populations),
            "alleles_square",
            (state_out[1], tile_out),
            (all_zero, all_one, *parts_of(both, "samp")),
        )
        tiles = (*parts_of(mix_tile, "samp"), *parts_of(all_tile, "var"))
        mix_zero, all_zero, prop, both = call(
            functools.partial(leap_kernel, populations),
            "leap",
            (*state_out, *sums_out),
            (mix_zero, all_zero, mix_one, all_one, mix_two, all_two, *tiles, alt, ref),
            turned,
        )
    (mixture,) = call(
        functools.partial(last_mixture_kernel, populations),
        "last_mixture",
        (((populations, samples), F32),),
        (mix_zero, twice, *all_parts_of(prop, "var")),
        moved=MIXTURE_COST,
    )
    (alleles,) = call(
        functools.partial(last_alleles_kernel, populations),
        "last_alleles",
        (((populations, variants), F32),),
        (all_zero, *parts_of(both, "samp")),
    )
    return mixture, alleles


def solution(mesh):
    placed = (P("samp", "var"), P("samp", "var"), P(None, "samp"), P(None, ("samp", "var")))
    return jax.shard_map(
        local,
        mesh=mesh,
        in_specs=placed,
        out_specs=(P(None, "samp"), P(None, "var")),
        check_vma=False,
    )
```

```python
import functools

import jax
import jax.numpy as jnp
from jax import lax
from jax.experimental import pallas as pl
from jax.experimental.pallas import tpu as pltpu
from jax.sharding import PartitionSpec as P

STEPS = 2
CLIP_LOW = 1e-05
NORM_EPS = 1e-10
F32 = jnp.float32
BF16 = jnp.bfloat16
SUBLANES = 8
LANES = 128
VMEM_BYTES = 40 * 2**20
TALL, WIDE = 512, 512
MIXTURE_COST = 5 * 10**9


def clip_unit(values):
    return jnp.clip(values, CLIP_LOW, 1.0 - CLIP_LOW)


def blocks_of(size, largest):
    width = min(size, largest)
    while size % width:
        width -= 1
    return width


def swap(value, axis, mask):
    size = lax.axis_size(axis)
    return lax.ppermute(value, axis, [(i, i ^ mask) for i in range(size)])


def strides_of(axis):
    return [1 << bit for bit in range(lax.axis_size(axis).bit_length() - 1)]


def all_parts_of(value, axis):
    return [value] + [swap(value, axis, mask) for mask in range(1, lax.axis_size(axis))]


def pair_sum(parts):
    while len(parts) > 1:
        parts = [a + b for a, b in zip(parts[::2], parts[1::2])]
    return parts[0]


def parts_of(value, axis):
    strides = strides_of(axis)
    for stride in strides[:-1]:
        value = value + swap(value, axis, stride)
    return value, swap(value, axis, strides[-1])


def gather_frequencies(frequencies):
    samp_count, var_count = lax.axis_size("samp"), lax.axis_size("var")
    group = samp_count // var_count
    samp, var = lax.axis_index("samp"), lax.axis_index("var")
    owner = samp // group
    both = ("samp", "var")
    arrived = [jnp.where(owner == var, frequencies, 0.0)]
    for mask in range(1, var_count):
        pairs = [
            (s * var_count + ((s // group) ^ mask), s * var_count + s // group)
            for s in range(samp_count)
        ]
        arrived.append(lax.ppermute(frequencies, both, pairs))
    stride = 1
    while stride < var_count:
        flip = (var & stride) != 0
        arrived = [jnp.where(flip, arrived[i ^ stride], arrived[i]) for i in range(var_count)]
        stride *= 2
    held = jnp.concatenate(arrived, axis=1)
    stride = 1
    while stride < group:
        other = swap(held, "samp", stride)
        upper = (samp & stride) != 0
        held = jnp.concatenate(
            [jnp.where(upper, other, held), jnp.where(upper, held, other)], axis=1
        )
        stride *= 2
    held = jnp.where(owner == var, held, 0.0)
    total = held
    for mask in range(1, var_count):
        pairs = [
            ((v * group + g) * var_count + v, ((v ^ mask) * group + g) * var_count + v)
            for v in range(var_count)
            for g in range(group)
        ]
        total = total + lax.ppermute(held, both, pairs)
    return total


def dot(left, right, left_dim, right_dim):
    return lax.dot_general(
        left, right, (((left_dim,), (right_dim,)), ((), ())), preferred_element_type=F32
    )


def split(values):
    high = values.astype(BF16)
    rest = values - high.astype(F32)
    middle = rest.astype(BF16)
    return high, middle, (rest - middle.astype(F32)).astype(BF16)


def two_terms(values):
    high = values.astype(BF16)
    return high, (values - high.astype(F32)).astype(BF16)


def row_mask(values, populations):
    rows = lax.broadcasted_iota(jnp.int32, values.shape, 0)
    return jnp.where(rows < populations, values, 0.0)


def pad_rows(values, rows):
    spare = jnp.zeros((rows - values.shape[0], values.shape[1]), values.dtype)
    return jnp.concatenate([values, spare], axis=0)


def put_packed(ref, first, stride, values):
    count = values.shape[0]
    for block in range(values.shape[1] // LANES):
        top = block * stride + first
        ref[top : top + count, :] = values[:, block * LANES : (block + 1) * LANES]


def sum_packed(parts, first, stride, count):
    pieces = []
    for top in range(first, parts[0].shape[0], stride):
        here = slice(top, top + count)
        pieces.append(pair_sum([part[here, :] for part in parts]))
    return jnp.concatenate(pieces, axis=1)


def expectation(
    populations, mixture, alleles, twice_here, alt_ref, ref_ref, prop_ref, both_ref, turned
):
    rows, samples = mixture.shape
    variants = alleles.shape[1]
    tall, wide = blocks_of(samples, TALL), blocks_of(variants, WIDE)
    mix_high, mix_mid, mix_low = split(mixture)
    all_high, all_mid, all_low = split(alleles)
    turned[...] = jnp.concatenate(
        [mix_high, mix_high, mix_mid, mix_mid, mix_high, mix_low], axis=0
    ).T
    right = jnp.concatenate([all_high, all_mid, all_high, all_mid, all_low, all_high], axis=0)
    toward = jnp.concatenate([all_high, all_mid], axis=0)
    left = jnp.concatenate([mix_high, mix_mid], axis=0)
    props = [jnp.zeros((2 * rows, tall), F32) for _ in range(0, samples, tall)]
    for start in range(0, variants, wide):
        across = slice(start, start + wide)
        excess = jnp.zeros((2 * rows, wide), F32)
        ref_sum = jnp.zeros((2 * rows, wide), F32)
        for index, top in enumerate(range(0, samples, tall)):
            here = slice(top, top + tall)
            expected = dot(turned[here, :], right[:, across], 1, 0)
            ref = ref_ref[here, across] * pl.reciprocal(1.0 - expected, approx=True)
            gap = alt_ref[here, across] * pl.reciprocal(expected, approx=True) - ref
            for term in two_terms(gap):
                props[index] = props[index] + dot(toward[:, across], term, 1, 1)
                excess = excess + dot(left[:, here], term, 1, 0)
            for term in two_terms(ref):
                ref_sum = ref_sum + dot(left[:, here], term, 1, 0)
        excess = excess[:populations] + excess[rows : rows + populations]
        ref_sum = ref_sum[:populations] + ref_sum[rows : rows + populations]
        first_block = start // LANES * 2 * populations
        put_packed(both_ref, first_block, 2 * populations, excess + ref_sum)
        put_packed(both_ref, first_block + populations, 2 * populations, ref_sum)
    prop = jnp.concatenate(props, axis=1)
    prop = prop[:populations] + prop[rows : rows + populations]
    along = jnp.sum(mixture[:populations] * prop, axis=0, keepdims=True)
    stride = prop_ref.shape[0] * LANES // samples
    put_packed(prop_ref, 0, stride, prop + (twice_here - along))
    if stride > populations:
        put_packed(prop_ref, populations, stride, twice_here)


def next_mixture(populations, mixture, twice_observed, prop_parts):
    rows, samples = mixture.shape
    stride = prop_parts[0].shape[0] * LANES // samples
    prop_sums = sum_packed(prop_parts, 0, stride, populations)
    if twice_observed is None:
        twice_observed = sum_packed(prop_parts, populations, stride, 1)
    moved = clip_unit(mixture[:populations] * prop_sums / twice_observed)
    return pad_rows(moved, rows), twice_observed


def next_alleles(populations, alleles, both_parts):
    alt_sums = sum_packed(both_parts, 0, 2 * populations, populations)
    ref_sums = sum_packed(both_parts, populations, 2 * populations, populations)
    current = alleles[:populations]
    weighted = current * alt_sums
    moved = clip_unit(weighted / (weighted + (1.0 - current) * ref_sums))
    return pad_rows(moved, alleles.shape[0])


def first_kernel(
    mixture, alleles, alt, ref, mixture_out, alleles_out, twice_out, prop_out, both_out, turned
):
    populations = mixture.shape[0]
    rows = mixture_out.shape[0]
    mix = pad_rows(mixture[...], rows)
    current = pad_rows(alleles[...], rows)
    mixture_out[...] = mix
    alleles_out[...] = current
    ones = jnp.ones((SUBLANES, alt.shape[1]), BF16)
    twice = dot(ones, (alt[...] + ref[...]).astype(BF16), 1, 1)[:1]
    twice_out[...] = twice
    expectation(populations, mix, current, twice, alt, ref, prop_out, both_out, turned)


def mixture_kernel(populations, with_twice, mixture, *refs):
    twice = refs[0][...] if with_twice else None
    prop_parts, outs = split_refs(refs[with_twice:], len(refs) - 2)
    mix, twice = next_mixture(populations, mixture[...], twice, prop_parts)
    outs[0][...] = mix
    if not with_twice:
        outs[1][...] = twice


def step_kernel(populations, mixture, alleles, twice_here, *refs):
    both_parts, (alt, ref, alleles_out, prop_out, both_out, turned) = split_refs(refs, 2)
    current = next_alleles(populations, alleles[...], both_parts)
    alleles_out[...] = current
    expectation(
        populations, mixture[...], current, twice_here[...], alt, ref, prop_out, both_out, turned
    )


def split_refs(refs, *counts):
    groups = []
    for count in counts:
        groups.append(refs[:count])
        refs = refs[count:]
    return (*groups, refs)


def folded(values):
    squares = values * values
    tile = squares.reshape(-1, SUBLANES, squares.shape[1]).sum(axis=0)
    width = tile.shape[1]
    return sum(tile[:, i : i + LANES] for i in range(0, width, LANES))


def squares(zero, one, two, tile):
    step = one - zero
    tile[:SUBLANES, :] = folded(step)
    tile[SUBLANES:, :] = folded(two - one - step)


def mixture_square_kernel(populations, zero, one, twice, *refs):
    prop_parts, (two_out, tile) = split_refs(refs, len(refs) - 2)
    two, _ = next_mixture(populations, one[...], twice[...], prop_parts)
    two_out[...] = two
    squares(zero[...], one[...], two, tile)


def alleles_square_kernel(populations, zero, one, *refs):
    both_parts, (two_out, tile) = split_refs(refs, 2)
    two = next_alleles(populations, one[...], both_parts)
    two_out[...] = two
    squares(zero[...], one[...], two, tile)


def leap(zero, one, two, tile):
    first = jnp.sum(tile[:SUBLANES], axis=(0, 1), keepdims=True)
    second = jnp.sum(tile[SUBLANES:], axis=(0, 1), keepdims=True)
    alpha = jnp.maximum(1.0, jnp.sqrt(first / (second + NORM_EPS)))
    step = one - zero
    curve = two - one - step
    return zero + 2.0 * alpha * step + alpha * alpha * curve


def leap_kernel(populations, *refs):
    states = [ref[...] for ref in refs[:6]]
    mix_zero, all_zero, mix_one, all_one, mix_two, all_two = states
    mix_parts, all_parts, rest = split_refs(refs[6:], 2, 2)
    twice_here, alt, ref, mixture_out, alleles_out, prop_out, both_out, turned = rest
    mix_tile = mix_parts[0][...] + mix_parts[1][...]
    all_tile = all_parts[0][...] + all_parts[1][...]
    clipped = row_mask(clip_unit(leap(mix_zero, mix_one, mix_two, mix_tile)), populations)
    mix = clipped / jnp.sum(clipped, axis=0, keepdims=True)
    current = row_mask(clip_unit(leap(all_zero, all_one, all_two, all_tile)), populations)
    mixture_out[...] = mix
    alleles_out[...] = current
    expectation(
        populations, mix, current, twice_here[...], alt, ref, prop_out, both_out, turned
    )


def last_mixture_kernel(populations, mixture, twice, *refs):
    prop_parts, (out,) = split_refs(refs, len(refs) - 1)
    mix, _ = next_mixture(populations, mixture[...], twice[...], prop_parts)
    out[...] = mix[:populations]


def last_alleles_kernel(populations, alleles, *refs):
    both_parts, (out,) = split_refs(refs, 2)
    out[...] = next_alleles(populations, alleles[...], both_parts)[:populations]


def call(kernel, name, outs, args, scratch=(), moved=0):
    whole = pl.BlockSpec(memory_space=pltpu.VMEM)
    cost = pl.CostEstimate(flops=moved, bytes_accessed=0, transcendentals=0) if moved else None
    return pl.pallas_call(
        kernel,
        out_shape=tuple(jax.ShapeDtypeStruct(*out) for out in outs),
        in_specs=[pl.BlockSpec(memory_space=pltpu.VMEM)] * len(args),
        out_specs=(whole,) * len(outs),
        scratch_shapes=list(scratch),
        compiler_params=pltpu.CompilerParams(vmem_limit_bytes=VMEM_BYTES),
        cost_estimate=cost,
        name=name,
    )(*args)


def local(genotypes, observed, proportions, frequencies):
    populations, samples = proportions.shape
    variants = genotypes.shape[1]
    rows = -(-populations // 16) * 16
    state_out = (((rows, samples), F32), ((rows, variants), F32))
    packed = populations * samples // LANES
    both_out = ((2 * populations * variants // LANES, LANES), F32)
    sums_out = (((packed, LANES), F32), both_out)
    first_sums_out = (((packed + samples // LANES, LANES), F32), both_out)
    tile_out = ((2 * SUBLANES, LANES), F32)
    turned = (pltpu.VMEM((samples, 6 * rows), BF16),)

    alleles = gather_frequencies(frequencies)
    alt = (observed * genotypes).astype(F32)
    ref = (observed * (2 - genotypes)).astype(F32)

    mix_zero, all_zero, twice_here, prop, both = call(
        first_kernel,
        "first",
        (*state_out, ((1, samples), F32), *first_sums_out),
        (proportions, alleles, alt, ref),
        turned,
    )

    def moved_mixture(mixture, twice, prop):
        known = () if twice is None else (twice,)
        extra = () if known else (((1, samples), F32),)
        out = call(
            functools.partial(mixture_kernel, populations, len(known)),
            "mixture",
            (state_out[0], *extra),
            (mixture, *known, *all_parts_of(prop, "var")),
            moved=MIXTURE_COST,
        )
        return out[0], (known or out[1:])[0]

    def step(mixture, alleles, both):
        return call(
            functools.partial(step_kernel, populations),
            "step",
            (state_out[1], *sums_out),
            (mixture, alleles, twice_here, *parts_of(both, "samp"), alt, ref),
            turned,
        )

    twice = None
    for repeat in range(STEPS):
        if repeat:
            mix_zero, twice = moved_mixture(mix_zero, twice, prop)
            all_zero, prop, both = step(mix_zero, all_zero, both)
        mix_one, twice = moved_mixture(mix_zero, twice, prop)
        all_one, prop, both = step(mix_one, all_zero, both)
        mix_two, mix_tile = call(
            functools.partial(mixture_square_kernel, populations),
            "mixture_square",
            (state_out[0], tile_out),
            (mix_zero, mix_one, twice, *all_parts_of(prop, "var")),
            moved=MIXTURE_COST,
        )
        all_two, all_tile = call(
            functools.partial(alleles_square_kernel, populations),
            "alleles_square",
            (state_out[1], tile_out),
            (all_zero, all_one, *parts_of(both, "samp")),
        )
        tiles = (*parts_of(mix_tile, "samp"), *parts_of(all_tile, "var"))
        mix_zero, all_zero, prop, both = call(
            functools.partial(leap_kernel, populations),
            "leap",
            (*state_out, *sums_out),
            (
                *(mix_zero, all_zero, mix_one, all_one, mix_two, all_two),
                *(*tiles, twice_here, alt, ref),
            ),
            turned,
        )
    (mixture,) = call(
        functools.partial(last_mixture_kernel, populations),
        "last_mixture",
        (((populations, samples), F32),),
        (mix_zero, twice, *all_parts_of(prop, "var")),
        moved=MIXTURE_COST,
    )
    (alleles,) = call(
        functools.partial(last_alleles_kernel, populations),
        "last_alleles",
        (((populations, variants), F32),),
        (all_zero, *parts_of(both, "samp")),
    )
    return mixture, alleles


def solution(mesh):
    placed = (P("samp", "var"), P("samp", "var"), P(None, "samp"), P(None, ("samp", "var")))
    return jax.shard_map(
        local,
        mesh=mesh,
        in_specs=placed,
        out_specs=(P(None, "samp"), P(None, "var")),
        check_vma=False,
    )
```

```python
import functools

import jax
import jax.numpy as jnp
from jax import lax
from jax.experimental import pallas as pl
from jax.experimental.pallas import tpu as pltpu
from jax.sharding import PartitionSpec as P

STEPS = 2
CLIP_LOW = 1e-05
NORM_EPS = 1e-10
F32 = jnp.float32
BF16 = jnp.bfloat16
SUBLANES = 8
LANES = 128
VMEM_BYTES = 32 * 2**20
TALL, WIDE = 512, 512
MIXTURE_COST = 5 * 10**9
ALLELES_COST = 5 * 10**9


def clip_unit(values):
    return jnp.clip(values, CLIP_LOW, 1.0 - CLIP_LOW)


def blocks_of(size, largest):
    width = min(size, largest)
    while size % width:
        width -= 1
    return width


def swap(value, axis, mask):
    size = lax.axis_size(axis)
    return lax.ppermute(value, axis, [(i, i ^ mask) for i in range(size)])


def strides_of(axis):
    return [1 << bit for bit in range(lax.axis_size(axis).bit_length() - 1)]


def all_parts_of(value, axis):
    return [value] + [swap(value, axis, mask) for mask in range(1, lax.axis_size(axis))]


def pair_sum(parts):
    while len(parts) > 1:
        parts = [a + b for a, b in zip(parts[::2], parts[1::2])]
    return parts[0]


def parts_of(value, axis):
    strides = strides_of(axis)
    for stride in strides[:-1]:
        value = value + swap(value, axis, stride)
    return value, swap(value, axis, strides[-1])


def gather_flags():
    samp_count, var_count = lax.axis_size("samp"), lax.axis_size("var")
    group = samp_count // var_count
    samp, var = lax.axis_index("samp"), lax.axis_index("var")
    var_bits = [(var & stride) != 0 for stride in strides_of("var")]
    samp_bits = [(samp & stride) != 0 for stride in strides_of("samp") if stride < group]
    return samp // group == var, var_bits, samp_bits


def gather_frequencies(frequencies, flags):
    owns, var_bits, samp_bits = flags
    samp_count, var_count = lax.axis_size("samp"), lax.axis_size("var")
    group = samp_count // var_count
    both = ("samp", "var")
    arrived = []
    for mask in range(1, var_count):
        pairs = [
            (s * var_count + ((s // group) ^ mask), s * var_count + s // group)
            for s in range(samp_count)
        ]
        arrived.append(lax.ppermute(frequencies, both, pairs))
    arrived = [jnp.where(owns, frequencies, 0.0)] + arrived
    for bit, flip in enumerate(var_bits):
        arrived = [jnp.where(flip, arrived[i ^ (1 << bit)], arrived[i]) for i in range(var_count)]
    held = jnp.concatenate(arrived, axis=1)
    for bit, upper in enumerate(samp_bits):
        other = swap(held, "samp", 1 << bit)
        held = jnp.concatenate(
            [jnp.where(upper, other, held), jnp.where(upper, held, other)], axis=1
        )
    held = jnp.where(owns, held, 0.0)
    total = held
    for mask in range(1, var_count):
        pairs = [
            ((v * group + g) * var_count + v, ((v ^ mask) * group + g) * var_count + v)
            for v in range(var_count)
            for g in range(group)
        ]
        total = total + lax.ppermute(held, both, pairs)
    return total


def dot(left, right, left_dim, right_dim):
    return lax.dot_general(
        left, right, (((left_dim,), (right_dim,)), ((), ())), preferred_element_type=F32
    )


def split(values):
    high = values.astype(BF16)
    rest = values - high.astype(F32)
    middle = rest.astype(BF16)
    return high, middle, (rest - middle.astype(F32)).astype(BF16)


def two_terms(values):
    high = values.astype(BF16)
    return high, (values - high.astype(F32)).astype(BF16)


def row_mask(values, populations):
    rows = lax.broadcasted_iota(jnp.int32, values.shape, 0)
    return jnp.where(rows < populations, values, 0.0)


def pad_rows(values, rows):
    spare = jnp.zeros((rows - values.shape[0], values.shape[1]), values.dtype)
    return jnp.concatenate([values, spare], axis=0)


def put_packed(ref, first, stride, values):
    count = values.shape[0]
    for block in range(values.shape[1] // LANES):
        top = block * stride + first
        ref[top : top + count, :] = values[:, block * LANES : (block + 1) * LANES]


def sum_packed(parts, first, stride, count):
    pieces = []
    for top in range(first, parts[0].shape[0], stride):
        here = slice(top, top + count)
        pieces.append(pair_sum([part[here, :] for part in parts]))
    return jnp.concatenate(pieces, axis=1)


def expectation(
    populations, mixture, alleles, twice_here, alt_ref, ref_ref, prop_ref, both_ref, turned
):
    rows, samples = mixture.shape
    variants = alleles.shape[1]
    tall, wide = blocks_of(samples, TALL), blocks_of(variants, WIDE)
    mix_high, mix_mid, mix_low = split(mixture)
    all_high, all_mid, all_low = split(alleles)
    turned[...] = jnp.concatenate(
        [mix_high, mix_high, mix_mid, mix_mid, mix_high, mix_low], axis=0
    ).T
    right = jnp.concatenate([all_high, all_mid, all_high, all_mid, all_low, all_high], axis=0)
    toward = jnp.concatenate([all_high, all_mid], axis=0)
    left = jnp.concatenate([mix_high, mix_mid], axis=0)
    props = [jnp.zeros((2 * rows, tall), F32) for _ in range(0, samples, tall)]
    for start in range(0, variants, wide):
        across = slice(start, start + wide)
        excess = jnp.zeros((2 * rows, wide), F32)
        ref_sum = jnp.zeros((2 * rows, wide), F32)
        for index, top in enumerate(range(0, samples, tall)):
            here = slice(top, top + tall)
            expected = dot(turned[here, :], right[:, across], 1, 0)
            ref = ref_ref[here, across] * pl.reciprocal(1.0 - expected, approx=True)
            gap = alt_ref[here, across] * pl.reciprocal(expected, approx=True) - ref
            for term in two_terms(gap):
                props[index] = props[index] + dot(toward[:, across], term, 1, 1)
                excess = excess + dot(left[:, here], term, 1, 0)
            for term in two_terms(ref):
                ref_sum = ref_sum + dot(left[:, here], term, 1, 0)
        excess = excess[:populations] + excess[rows : rows + populations]
        ref_sum = ref_sum[:populations] + ref_sum[rows : rows + populations]
        first_block = start // LANES * 2 * populations
        put_packed(both_ref, first_block, 2 * populations, excess + ref_sum)
        put_packed(both_ref, first_block + populations, 2 * populations, ref_sum)
    prop = jnp.concatenate(props, axis=1)
    prop = prop[:populations] + prop[rows : rows + populations]
    along = jnp.sum(mixture[:populations] * prop, axis=0, keepdims=True)
    stride = prop_ref.shape[0] * LANES // samples
    put_packed(prop_ref, 0, stride, prop + (twice_here - along))
    if stride > populations:
        put_packed(prop_ref, populations, stride, twice_here)


def next_mixture(populations, mixture, twice_observed, prop_parts):
    rows, samples = mixture.shape
    stride = prop_parts[0].shape[0] * LANES // samples
    prop_sums = sum_packed(prop_parts, 0, stride, populations)
    if twice_observed is None:
        twice_observed = sum_packed(prop_parts, populations, stride, 1)
    moved = clip_unit(mixture[:populations] * prop_sums / twice_observed)
    return pad_rows(moved, rows), twice_observed


def next_alleles(populations, alleles, both_parts):
    alt_sums = sum_packed(both_parts, 0, 2 * populations, populations)
    ref_sums = sum_packed(both_parts, populations, 2 * populations, populations)
    current = alleles[:populations]
    weighted = current * alt_sums
    moved = clip_unit(weighted / (weighted + (1.0 - current) * ref_sums))
    return pad_rows(moved, alleles.shape[0])


def prepare_kernel(genotypes, observed, alt_out, ref_out, twice_out, landed, arrivals):
    samples, variants = genotypes.shape
    tall = samples // arrivals.shape[1]
    copies = []
    for index, top in enumerate(range(0, samples, tall)):
        here = pl.ds(top, tall)
        for place, source in enumerate((genotypes, observed)):
            copy = pltpu.make_async_copy(
                source.at[here, :], landed.at[place, here, :], arrivals.at[place, index]
            )
            copy.start()
            copies.append(copy)
    ones = jnp.ones((SUBLANES, variants), BF16)
    for index, top in enumerate(range(0, samples, tall)):
        here = slice(top, top + tall)
        copies[2 * index].wait()
        copies[2 * index + 1].wait()
        seen = landed[1, here, :].astype(F32)
        alt = seen * landed[0, here, :].astype(F32)
        alt_out[here, :] = alt
        ref_out[here, :] = 2.0 * seen - alt
        twice_out[:, here] = 2.0 * dot(ones, seen.astype(BF16), 1, 1)[:1]


def first_kernel(
    mixture, alleles, twice_here, alt, ref, mixture_out, alleles_out, prop_out, both_out, turned
):
    populations = mixture.shape[0]
    rows = mixture_out.shape[0]
    mix = pad_rows(mixture[...], rows)
    current = pad_rows(alleles[...], rows)
    mixture_out[...] = mix
    alleles_out[...] = current
    expectation(
        populations, mix, current, twice_here[...], alt, ref, prop_out, both_out, turned
    )


def mixture_kernel(populations, with_twice, mixture, *refs):
    twice = refs[0][...] if with_twice else None
    prop_parts, outs = split_refs(refs[with_twice:], len(refs) - 2)
    mix, twice = next_mixture(populations, mixture[...], twice, prop_parts)
    outs[0][...] = mix
    if not with_twice:
        outs[1][...] = twice


def step_kernel(populations, mixture, alleles, twice_here, *refs):
    both_parts, (alt, ref, alleles_out, prop_out, both_out, turned) = split_refs(refs, 2)
    current = next_alleles(populations, alleles[...], both_parts)
    alleles_out[...] = current
    expectation(
        populations, mixture[...], current, twice_here[...], alt, ref, prop_out, both_out, turned
    )


def split_refs(refs, *counts):
    groups = []
    for count in counts:
        groups.append(refs[:count])
        refs = refs[count:]
    return (*groups, refs)


def folded(values):
    squares = values * values
    tile = squares.reshape(-1, SUBLANES, squares.shape[1]).sum(axis=0)
    width = tile.shape[1]
    return sum(tile[:, i : i + LANES] for i in range(0, width, LANES))


def squares(zero, one, two, tile):
    step = one - zero
    tile[:SUBLANES, :] = folded(step)
    tile[SUBLANES:, :] = folded(two - one - step)


def mixture_square_kernel(populations, zero, one, twice, *refs):
    prop_parts, (two_out, tile) = split_refs(refs, len(refs) - 2)
    two, _ = next_mixture(populations, one[...], twice[...], prop_parts)
    two_out[...] = two
    squares(zero[...], one[...], two, tile)


def alleles_square_kernel(populations, zero, one, *refs):
    both_parts, (two_out, tile) = split_refs(refs, 2)
    two = next_alleles(populations, one[...], both_parts)
    two_out[...] = two
    squares(zero[...], one[...], two, tile)


def leap(zero, one, two, tile):
    first = jnp.sum(tile[:SUBLANES], axis=(0, 1), keepdims=True)
    second = jnp.sum(tile[SUBLANES:], axis=(0, 1), keepdims=True)
    alpha = jnp.maximum(1.0, jnp.sqrt(first / (second + NORM_EPS)))
    step = one - zero
    curve = two - one - step
    return zero + 2.0 * alpha * step + alpha * alpha * curve


def leap_kernel(populations, *refs):
    states = [ref[...] for ref in refs[:6]]
    mix_zero, all_zero, mix_one, all_one, mix_two, all_two = states
    mix_parts, all_parts, rest = split_refs(refs[6:], 2, 2)
    twice_here, alt, ref, mixture_out, alleles_out, prop_out, both_out, turned = rest
    mix_tile = mix_parts[0][...] + mix_parts[1][...]
    all_tile = all_parts[0][...] + all_parts[1][...]
    clipped = row_mask(clip_unit(leap(mix_zero, mix_one, mix_two, mix_tile)), populations)
    mix = clipped / jnp.sum(clipped, axis=0, keepdims=True)
    current = row_mask(clip_unit(leap(all_zero, all_one, all_two, all_tile)), populations)
    mixture_out[...] = mix
    alleles_out[...] = current
    expectation(
        populations, mix, current, twice_here[...], alt, ref, prop_out, both_out, turned
    )


def last_kernel(populations, mixture, alleles, *refs):
    both_parts, (mixture_out, alleles_out) = split_refs(refs, 2)
    mixture_out[...] = mixture[:populations, :]
    alleles_out[...] = next_alleles(populations, alleles[...], both_parts)[:populations]


def call(kernel, name, outs, args, scratch=(), flops=0):
    whole = pl.BlockSpec(memory_space=pltpu.VMEM)
    cost = pl.CostEstimate(flops=flops, bytes_accessed=0, transcendentals=0) if flops else None
    return pl.pallas_call(
        kernel,
        out_shape=tuple(jax.ShapeDtypeStruct(*out) for out in outs),
        in_specs=[pl.BlockSpec(memory_space=pltpu.VMEM)] * len(args),
        out_specs=(whole,) * len(outs),
        scratch_shapes=list(scratch),
        compiler_params=pltpu.CompilerParams(vmem_limit_bytes=VMEM_BYTES),
        cost_estimate=cost,
        name=name,
    )(*args)


def local(genotypes, observed, proportions, frequencies):
    populations, samples = proportions.shape
    variants = genotypes.shape[1]
    rows = -(-populations // 16) * 16
    state_out = (((rows, samples), F32), ((rows, variants), F32))
    packed = populations * samples // LANES
    both_out = ((2 * populations * variants // LANES, LANES), F32)
    sums_out = (((packed, LANES), F32), both_out)
    first_sums_out = (((packed + samples // LANES, LANES), F32), both_out)
    tile_out = ((2 * SUBLANES, LANES), F32)
    turned = (pltpu.VMEM((samples, 6 * rows), BF16),)

    chunks = samples // blocks_of(samples, 128)
    flags, genotypes, observed = lax.optimization_barrier((gather_flags(), genotypes, observed))
    in_place = [
        pltpu.with_memory_space_constraint(array, pltpu.HBM) for array in (genotypes, observed)
    ]
    whole = pl.BlockSpec(memory_space=pltpu.VMEM)
    alt, ref, twice_here = pl.pallas_call(
        prepare_kernel,
        out_shape=(
            pltpu.VMEM((samples, variants), F32),
            pltpu.VMEM((samples, variants), F32),
            jax.ShapeDtypeStruct((1, samples), F32),
        ),
        in_specs=[pl.BlockSpec(memory_space=pltpu.HBM)] * 2,
        out_specs=(whole,) * 3,
        scratch_shapes=[
            pltpu.VMEM((2, samples, variants), jnp.int32),
            pltpu.SemaphoreType.DMA((2, chunks)),
        ],
        compiler_params=pltpu.CompilerParams(vmem_limit_bytes=VMEM_BYTES),
        name="prepare",
    )(*in_place)
    alleles = gather_frequencies(frequencies, flags)

    mix_zero, all_zero, prop, both = call(
        first_kernel,
        "first",
        (*state_out, *first_sums_out),
        (proportions, alleles, twice_here, alt, ref),
        turned,
    )

    def moved_mixture(mixture, twice, prop):
        known = () if twice is None else (twice,)
        extra = () if known else (((1, samples), F32),)
        out = call(
            functools.partial(mixture_kernel, populations, len(known)),
            "mixture",
            (state_out[0], *extra),
            (mixture, *known, *all_parts_of(prop, "var")),
            flops=MIXTURE_COST,
        )
        return out[0], (known or out[1:])[0]

    def step(mixture, alleles, both):
        return call(
            functools.partial(step_kernel, populations),
            "step",
            (state_out[1], *sums_out),
            (mixture, alleles, twice_here, *parts_of(both, "samp"), alt, ref),
            turned,
        )

    twice = None
    for repeat in range(STEPS):
        if repeat:
            mix_zero, twice = moved_mixture(mix_zero, twice, prop)
            all_zero, prop, both = step(mix_zero, all_zero, both)
        mix_one, twice = moved_mixture(mix_zero, twice, prop)
        all_one, prop, both = step(mix_one, all_zero, both)
        mix_two, mix_tile = call(
            functools.partial(mixture_square_kernel, populations),
            "mixture_square",
            (state_out[0], tile_out),
            (mix_zero, mix_one, twice, *all_parts_of(prop, "var")),
            flops=MIXTURE_COST,
        )
        all_two, all_tile = call(
            functools.partial(alleles_square_kernel, populations),
            "alleles_square",
            (state_out[1], tile_out),
            (all_zero, all_one, *parts_of(both, "samp")),
            flops=ALLELES_COST,
        )
        tiles = (*parts_of(mix_tile, "samp"), *parts_of(all_tile, "var"))
        mix_zero, all_zero, prop, both = call(
            functools.partial(leap_kernel, populations),
            "leap",
            (*state_out, *sums_out),
            (
                *(mix_zero, all_zero, mix_one, all_one, mix_two, all_two),
                *(*tiles, twice_here, alt, ref),
            ),
            turned,
        )
    mixture, _ = moved_mixture(mix_zero, twice, prop)
    return call(
        functools.partial(last_kernel, populations),
        "last",
        (((populations, samples), F32), ((populations, variants), F32)),
        (mixture, all_zero, *parts_of(both, "samp")),
    )


def solution(mesh):
    placed = (P("samp", "var"), P("samp", "var"), P(None, "samp"), P(None, ("samp", "var")))
    return jax.shard_map(
        local,
        mesh=mesh,
        in_specs=placed,
        out_specs=(P(None, "samp"), P(None, "var")),
        check_vma=False,
    )
```

```python
import functools

import jax
import jax.numpy as jnp
from jax import lax
from jax.experimental import pallas as pl
from jax.experimental.pallas import tpu as pltpu
from jax.sharding import PartitionSpec as P

STEPS = 2
CLIP_LOW = 1e-05
NORM_EPS = 1e-10
F32 = jnp.float32
BF16 = jnp.bfloat16
SUBLANES = 8
LANES = 128
VMEM_BYTES = 32 * 2**20
TALL, WIDE = 512, 512
MIXTURE_COST = 5 * 10**9
ALLELES_COST = 5 * 10**9


def clip_unit(values):
    return jnp.clip(values, CLIP_LOW, 1.0 - CLIP_LOW)


def blocks_of(size, largest):
    width = min(size, largest)
    while size % width:
        width -= 1
    return width


def swap(value, axis, mask):
    size = lax.axis_size(axis)
    return lax.ppermute(value, axis, [(i, i ^ mask) for i in range(size)])


def strides_of(axis):
    return [1 << bit for bit in range(lax.axis_size(axis).bit_length() - 1)]


def all_parts_of(value, axis):
    return [value] + [swap(value, axis, mask) for mask in range(1, lax.axis_size(axis))]


def pair_sum(parts):
    while len(parts) > 1:
        parts = [a + b for a, b in zip(parts[::2], parts[1::2])]
    return parts[0]


def parts_of(value, axis, done=0):
    strides = strides_of(axis)[done:]
    for stride in strides[:-1]:
        value = value + swap(value, axis, stride)
    return value, swap(value, axis, strides[-1])


def gather_flags():
    samp_count, var_count = lax.axis_size("samp"), lax.axis_size("var")
    group = samp_count // var_count
    samp, var = lax.axis_index("samp"), lax.axis_index("var")
    var_bits = [(var & stride) != 0 for stride in strides_of("var")]
    samp_bits = [(samp & stride) != 0 for stride in strides_of("samp") if stride < group]
    return samp // group == var, var_bits, samp_bits


def gather_frequencies(frequencies, flags):
    owns, var_bits, samp_bits = flags
    samp_count, var_count = lax.axis_size("samp"), lax.axis_size("var")
    group = samp_count // var_count
    both = ("samp", "var")
    arrived = []
    for mask in range(1, var_count):
        pairs = [
            (s * var_count + ((s // group) ^ mask), s * var_count + s // group)
            for s in range(samp_count)
        ]
        arrived.append(lax.ppermute(frequencies, both, pairs))
    arrived = [jnp.where(owns, frequencies, 0.0)] + arrived
    for bit, flip in enumerate(var_bits):
        arrived = [jnp.where(flip, arrived[i ^ (1 << bit)], arrived[i]) for i in range(var_count)]
    held = jnp.concatenate(arrived, axis=1)
    for bit, upper in enumerate(samp_bits):
        other = swap(held, "samp", 1 << bit)
        held = jnp.concatenate(
            [jnp.where(upper, other, held), jnp.where(upper, held, other)], axis=1
        )
    held = jnp.where(owns, held, 0.0)
    total = held
    for mask in range(1, var_count):
        pairs = [
            ((v * group + g) * var_count + v, ((v ^ mask) * group + g) * var_count + v)
            for v in range(var_count)
            for g in range(group)
        ]
        total = total + lax.ppermute(held, both, pairs)
    return total


def dot(left, right, left_dim, right_dim):
    return lax.dot_general(
        left, right, (((left_dim,), (right_dim,)), ((), ())), preferred_element_type=F32
    )


def split(values):
    high = values.astype(BF16)
    rest = values - high.astype(F32)
    middle = rest.astype(BF16)
    return high, middle, (rest - middle.astype(F32)).astype(BF16)


def two_terms(values):
    high = values.astype(BF16)
    return high, (values - high.astype(F32)).astype(BF16)


def row_mask(values, populations):
    rows = lax.broadcasted_iota(jnp.int32, values.shape, 0)
    return jnp.where(rows < populations, values, 0.0)


def pad_rows(values, rows):
    spare = jnp.zeros((rows - values.shape[0], values.shape[1]), values.dtype)
    return jnp.concatenate([values, spare], axis=0)


def put_packed(ref, first, stride, values):
    count = values.shape[0]
    for block in range(values.shape[1] // LANES):
        top = block * stride + first
        ref[top : top + count, :] = values[:, block * LANES : (block + 1) * LANES]


def sum_packed(parts, first, stride, count):
    pieces = []
    for top in range(first, parts[0].shape[0], stride):
        here = slice(top, top + count)
        pieces.append(pair_sum([part[here, :] for part in parts]))
    return jnp.concatenate(pieces, axis=1)


def variant_sums(
    populations, mixture, alleles, alt_ref, ref_ref, both_ref, gap_high, gap_low, turned
):
    rows, samples = mixture.shape
    variants = alleles.shape[1]
    tall, wide = blocks_of(samples, TALL), blocks_of(variants, WIDE)
    mix_high, mix_mid, mix_low = split(mixture)
    all_high, all_mid, all_low = split(alleles)
    turned[...] = jnp.concatenate(
        [mix_high, mix_high, mix_mid, mix_mid, mix_high, mix_low], axis=0
    ).T
    right = jnp.concatenate([all_high, all_mid, all_high, all_mid, all_low, all_high], axis=0)
    left = jnp.concatenate([mix_high, mix_mid], axis=0)
    for start in range(0, variants, wide):
        across = slice(start, start + wide)
        excess = jnp.zeros((2 * rows, wide), F32)
        ref_sum = jnp.zeros((2 * rows, wide), F32)
        for top in range(0, samples, tall):
            here = slice(top, top + tall)
            expected = dot(turned[here, :], right[:, across], 1, 0)
            ref = ref_ref[here, across] * pl.reciprocal(1.0 - expected, approx=True)
            gap = alt_ref[here, across] * pl.reciprocal(expected, approx=True) - ref
            for table, term in zip((gap_high, gap_low), two_terms(gap)):
                table[here, across] = term
                excess = excess + dot(left[:, here], term, 1, 0)
            for term in two_terms(ref):
                ref_sum = ref_sum + dot(left[:, here], term, 1, 0)
        excess = excess[:populations] + excess[rows : rows + populations]
        ref_sum = ref_sum[:populations] + ref_sum[rows : rows + populations]
        first_block = start // LANES * 2 * populations
        put_packed(both_ref, first_block, 2 * populations, excess + ref_sum)
        put_packed(both_ref, first_block + populations, 2 * populations, ref_sum)


def sample_sums_kernel(populations, mixture, alleles, twice_here, gap_high, gap_low, prop_ref):
    samples = mixture.shape[1]
    rows = alleles.shape[0]
    all_high, all_mid, _ = split(alleles[...])
    toward = jnp.concatenate([all_high, all_mid], axis=0)
    prop = dot(toward, gap_high[...], 1, 1) + dot(toward, gap_low[...], 1, 1)
    prop = prop[:populations] + prop[rows : rows + populations]
    along = jnp.sum(mixture[:populations, :] * prop, axis=0, keepdims=True)
    stride = prop_ref.shape[0] * LANES // samples
    put_packed(prop_ref, 0, stride, prop + (twice_here[...] - along))
    if stride > populations:
        put_packed(prop_ref, populations, stride, twice_here[...])


def next_mixture(populations, mixture, twice_observed, prop_parts):
    rows, samples = mixture.shape
    stride = prop_parts[0].shape[0] * LANES // samples
    prop_sums = sum_packed(prop_parts, 0, stride, populations)
    if twice_observed is None:
        twice_observed = sum_packed(prop_parts, populations, stride, 1)
    moved = clip_unit(mixture[:populations] * prop_sums / twice_observed)
    return pad_rows(moved, rows), twice_observed


def next_alleles(populations, alleles, both_parts):
    alt_sums = sum_packed(both_parts, 0, 2 * populations, populations)
    ref_sums = sum_packed(both_parts, populations, 2 * populations, populations)
    current = alleles[:populations]
    weighted = current * alt_sums
    moved = clip_unit(weighted / (weighted + (1.0 - current) * ref_sums))
    return pad_rows(moved, alleles.shape[0])


def prepare_kernel(genotypes, observed, alt_out, ref_out, twice_out, landed, arrivals):
    samples, variants = genotypes.shape
    tall = samples // arrivals.shape[1]
    copies = []
    for index, top in enumerate(range(0, samples, tall)):
        here = pl.ds(top, tall)
        for place, source in enumerate((genotypes, observed)):
            copy = pltpu.make_async_copy(
                source.at[here, :], landed.at[place, here, :], arrivals.at[place, index]
            )
            copy.start()
            copies.append(copy)
    ones = jnp.ones((SUBLANES, variants), BF16)
    for index, top in enumerate(range(0, samples, tall)):
        here = slice(top, top + tall)
        copies[2 * index].wait()
        copies[2 * index + 1].wait()
        seen = landed[1, here, :].astype(F32)
        alt = seen * landed[0, here, :].astype(F32)
        alt_out[here, :] = alt
        ref_out[here, :] = 2.0 * seen - alt
        twice_out[:, here] = 2.0 * dot(ones, seen.astype(BF16), 1, 1)[:1]


def first_kernel(mixture, alleles, alt, ref, mixture_out, alleles_out, both_out, *refs):
    populations = mixture.shape[0]
    rows = mixture_out.shape[0]
    mix = pad_rows(mixture[...], rows)
    current = pad_rows(alleles[...], rows)
    mixture_out[...] = mix
    alleles_out[...] = current
    variant_sums(populations, mix, current, alt, ref, both_out, *refs)


def mixture_kernel(populations, with_twice, mixture, *refs):
    twice = refs[0][...] if with_twice else None
    prop_parts, outs = split_refs(refs[with_twice:], len(refs) - 2)
    mix, twice = next_mixture(populations, mixture[...], twice, prop_parts)
    outs[0][...] = mix
    if not with_twice:
        outs[1][...] = twice


def step_kernel(populations, mixture, alleles, *refs):
    both_parts, (alt, ref, alleles_out, both_out), refs = split_refs(refs, 2, 4)
    current = next_alleles(populations, alleles[...], both_parts)
    alleles_out[...] = current
    variant_sums(populations, mixture[...], current, alt, ref, both_out, *refs)


def split_refs(refs, *counts):
    groups = []
    for count in counts:
        groups.append(refs[:count])
        refs = refs[count:]
    return (*groups, refs)


def folded(values):
    squares = values * values
    tile = squares.reshape(-1, SUBLANES, squares.shape[1]).sum(axis=0)
    width = tile.shape[1]
    return sum(tile[:, i : i + LANES] for i in range(0, width, LANES))


def squares(zero, one, two, tile):
    step = one - zero
    tile[:SUBLANES, :] = folded(step)
    tile[SUBLANES:, :] = folded(two - one - step)


def mixture_square_kernel(populations, zero, one, twice, *refs):
    prop_parts, (two_out, tile) = split_refs(refs, len(refs) - 2)
    two, _ = next_mixture(populations, one[...], twice[...], prop_parts)
    two_out[...] = two
    squares(zero[...], one[...], two, tile)


def alleles_square_kernel(populations, zero, one, *refs):
    both_parts, (two_out, tile) = split_refs(refs, 2)
    two = next_alleles(populations, one[...], both_parts)
    two_out[...] = two
    squares(zero[...], one[...], two, tile)


def leap(zero, one, two, tile):
    first = jnp.sum(tile[:SUBLANES], axis=(0, 1), keepdims=True)
    second = jnp.sum(tile[SUBLANES:], axis=(0, 1), keepdims=True)
    alpha = jnp.maximum(1.0, jnp.sqrt(first / (second + NORM_EPS)))
    step = one - zero
    curve = two - one - step
    return zero + 2.0 * alpha * step + alpha * alpha * curve


def leap_kernel(populations, *refs):
    states = [ref[...] for ref in refs[:6]]
    mix_zero, all_zero, mix_one, all_one, mix_two, all_two = states
    mix_parts, all_parts, rest = split_refs(refs[6:], 2, 2)
    alt, ref, mixture_out, alleles_out, both_out, *refs = rest
    mix_tile = mix_parts[0][...] + mix_parts[1][...]
    all_tile = all_parts[0][...] + all_parts[1][...]
    clipped = row_mask(clip_unit(leap(mix_zero, mix_one, mix_two, mix_tile)), populations)
    mix = clipped / jnp.sum(clipped, axis=0, keepdims=True)
    current = row_mask(clip_unit(leap(all_zero, all_one, all_two, all_tile)), populations)
    mixture_out[...] = mix
    alleles_out[...] = current
    variant_sums(populations, mix, current, alt, ref, both_out, *refs)


def last_kernel(populations, mixture, alleles, *refs):
    both_parts, (mixture_out, alleles_out) = split_refs(refs, 2)
    mixture_out[...] = mixture[:populations, :]
    alleles_out[...] = next_alleles(populations, alleles[...], both_parts)[:populations]


def call(kernel, name, outs, args, scratch=(), flops=0):
    whole = pl.BlockSpec(memory_space=pltpu.VMEM)
    cost = pl.CostEstimate(flops=flops, bytes_accessed=0, transcendentals=0) if flops else None
    return pl.pallas_call(
        kernel,
        out_shape=tuple(jax.ShapeDtypeStruct(*out) for out in outs),
        in_specs=[pl.BlockSpec(memory_space=pltpu.VMEM)] * len(args),
        out_specs=(whole,) * len(outs),
        scratch_shapes=list(scratch),
        compiler_params=pltpu.CompilerParams(vmem_limit_bytes=VMEM_BYTES),
        cost_estimate=cost,
        name=name,
    )(*args)


def local(genotypes, observed, proportions, frequencies):
    populations, samples = proportions.shape
    variants = genotypes.shape[1]
    rows = -(-populations // 16) * 16
    state_out = (((rows, samples), F32), ((rows, variants), F32))
    packed = populations * samples // LANES
    both_out = ((2 * populations * variants // LANES, LANES), F32)
    sums_out = (both_out, ((samples, variants), BF16), ((samples, variants), BF16))
    tile_out = ((2 * SUBLANES, LANES), F32)
    turned = (pltpu.VMEM((samples, 6 * rows), BF16),)

    chunks = samples // blocks_of(samples, 128)
    flags, genotypes, observed = lax.optimization_barrier((gather_flags(), genotypes, observed))
    in_place = [
        pltpu.with_memory_space_constraint(array, pltpu.HBM) for array in (genotypes, observed)
    ]
    whole = pl.BlockSpec(memory_space=pltpu.VMEM)
    alt, ref, twice_here = pl.pallas_call(
        prepare_kernel,
        out_shape=(
            pltpu.VMEM((samples, variants), F32),
            pltpu.VMEM((samples, variants), F32),
            jax.ShapeDtypeStruct((1, samples), F32),
        ),
        in_specs=[pl.BlockSpec(memory_space=pltpu.HBM)] * 2,
        out_specs=(whole,) * 3,
        scratch_shapes=[
            pltpu.VMEM((2, samples, variants), jnp.int32),
            pltpu.SemaphoreType.DMA((2, chunks)),
        ],
        compiler_params=pltpu.CompilerParams(vmem_limit_bytes=VMEM_BYTES),
        name="prepare",
    )(*in_place)
    alleles = gather_frequencies(frequencies, flags)

    def sums(mixture, alleles, both, gaps, extra=0):
        (prop,) = call(
            functools.partial(sample_sums_kernel, populations),
            "sample_sums",
            (((packed + extra, LANES), F32),),
            (mixture, alleles, twice_here, *gaps),
        )
        both = both + swap(both, "samp", 1)
        return lax.optimization_barrier((prop, both))

    mix_zero, all_zero, both, *gaps = call(
        first_kernel,
        "first",
        (*state_out, *sums_out),
        (proportions, alleles, alt, ref),
        turned,
    )
    prop, both = sums(mix_zero, all_zero, both, gaps, samples // LANES)

    def moved_mixture(mixture, twice, prop):
        known = () if twice is None else (twice,)
        extra = () if known else (((1, samples), F32),)
        out = call(
            functools.partial(mixture_kernel, populations, len(known)),
            "mixture",
            (state_out[0], *extra),
            (mixture, *known, *all_parts_of(prop, "var")),
            flops=MIXTURE_COST,
        )
        return out[0], (known or out[1:])[0]

    def step(mixture, alleles, both):
        moved, both, *gaps = call(
            functools.partial(step_kernel, populations),
            "step",
            (state_out[1], *sums_out),
            (mixture, alleles, *parts_of(both, "samp", 1), alt, ref),
            turned,
        )
        return moved, *sums(mixture, moved, both, gaps)

    twice = None
    for repeat in range(STEPS):
        if repeat:
            mix_zero, twice = moved_mixture(mix_zero, twice, prop)
            all_zero, prop, both = step(mix_zero, all_zero, both)
        mix_one, twice = moved_mixture(mix_zero, twice, prop)
        all_one, prop, both = step(mix_one, all_zero, both)
        mix_two, mix_tile = call(
            functools.partial(mixture_square_kernel, populations),
            "mixture_square",
            (state_out[0], tile_out),
            (mix_zero, mix_one, twice, *all_parts_of(prop, "var")),
            flops=MIXTURE_COST,
        )
        all_two, all_tile = call(
            functools.partial(alleles_square_kernel, populations),
            "alleles_square",
            (state_out[1], tile_out),
            (all_zero, all_one, *parts_of(both, "samp", 1)),
            flops=ALLELES_COST,
        )
        mix_tile = mix_tile + swap(mix_tile, "samp", 1)
        mix_tile, all_tile = lax.optimization_barrier((mix_tile, all_tile))
        tiles = (*parts_of(mix_tile, "samp", 1), *parts_of(all_tile, "var"))
        mix_zero, all_zero, both, *gaps = call(
            functools.partial(leap_kernel, populations),
            "leap",
            (*state_out, *sums_out),
            (mix_zero, all_zero, mix_one, all_one, mix_two, all_two, *tiles, alt, ref),
            turned,
        )
        prop, both = sums(mix_zero, all_zero, both, gaps)
    mixture, _ = moved_mixture(mix_zero, twice, prop)
    return call(
        functools.partial(last_kernel, populations),
        "last",
        (((populations, samples), F32), ((populations, variants), F32)),
        (mixture, all_zero, *parts_of(both, "samp", 1)),
    )


def solution(mesh):
    placed = (P("samp", "var"), P("samp", "var"), P(None, "samp"), P(None, ("samp", "var")))
    return jax.shard_map(
        local,
        mesh=mesh,
        in_specs=placed,
        out_specs=(P(None, "samp"), P(None, "var")),
        check_vma=False,
    )
```

```python
import functools

import jax
import jax.numpy as jnp
from jax import lax
from jax.experimental import pallas as pl
from jax.experimental.pallas import tpu as pltpu
from jax.sharding import PartitionSpec as P

STEPS = 2
CLIP_LOW = 1e-05
NORM_EPS = 1e-10
F32 = jnp.float32
BF16 = jnp.bfloat16
SUBLANES = 8
LANES = 128
VMEM_BYTES = 32 * 2**20
TALL, WIDE = 512, 1024
MIXTURE_COST = 5 * 10**9
ALLELES_COST = 5 * 10**9


def clip_unit(values):
    return jnp.clip(values, CLIP_LOW, 1.0 - CLIP_LOW)


def blocks_of(size, largest):
    width = min(size, largest)
    while size % width:
        width -= 1
    return width


def swap(value, axis, mask):
    size = lax.axis_size(axis)
    return lax.ppermute(value, axis, [(i, i ^ mask) for i in range(size)])


def strides_of(axis):
    return [1 << bit for bit in range(lax.axis_size(axis).bit_length() - 1)]


def all_parts_of(value, axis):
    return [value] + [swap(value, axis, i ^ (i >> 1)) for i in range(1, lax.axis_size(axis))]


def pair_sum(parts):
    while len(parts) > 1:
        parts = [a + b for a, b in zip(parts[::2], parts[1::2])]
    return parts[0]


def parts_of(value, axis, done=0):
    strides = strides_of(axis)[done:]
    for stride in strides[:-1]:
        value = value + swap(value, axis, stride)
    return value, swap(value, axis, strides[-1])


def gather_flags():
    samp_count, var_count = lax.axis_size("samp"), lax.axis_size("var")
    group = samp_count // var_count
    samp, var = lax.axis_index("samp"), lax.axis_index("var")
    var_bits = [(var & stride) != 0 for stride in strides_of("var")]
    samp_bits = [(samp & stride) != 0 for stride in strides_of("samp") if stride < group]
    return samp // group == var, var_bits, samp_bits


def gather_frequencies(frequencies, flags):
    owns, var_bits, samp_bits = flags
    samp_count, var_count = lax.axis_size("samp"), lax.axis_size("var")
    group = samp_count // var_count
    both = ("samp", "var")
    arrived = []
    for mask in range(1, var_count):
        pairs = [
            (s * var_count + ((s // group) ^ mask), s * var_count + s // group)
            for s in range(samp_count)
        ]
        arrived.append(lax.ppermute(frequencies, both, pairs))
    arrived = [jnp.where(owns, frequencies, 0.0)] + arrived
    for bit, flip in enumerate(var_bits):
        arrived = [jnp.where(flip, arrived[i ^ (1 << bit)], arrived[i]) for i in range(var_count)]
    held = jnp.concatenate(arrived, axis=1)
    for bit, upper in enumerate(samp_bits):
        other = swap(held, "samp", 1 << bit)
        held = jnp.concatenate(
            [jnp.where(upper, other, held), jnp.where(upper, held, other)], axis=1
        )
    held = jnp.where(owns, held, 0.0)
    total = held
    for mask in range(1, var_count):
        pairs = [
            ((v * group + g) * var_count + v, ((v ^ mask) * group + g) * var_count + v)
            for v in range(var_count)
            for g in range(group)
        ]
        total = total + lax.ppermute(held, both, pairs)
    return total


def dot(left, right, left_dim, right_dim):
    return lax.dot_general(
        left, right, (((left_dim,), (right_dim,)), ((), ())), preferred_element_type=F32
    )


def split(values):
    high = values.astype(BF16)
    rest = values - high.astype(F32)
    middle = rest.astype(BF16)
    return high, middle, (rest - middle.astype(F32)).astype(BF16)


def two_terms(values):
    high = values.astype(BF16)
    return high, (values - high.astype(F32)).astype(BF16)


def row_mask(values, populations):
    rows = lax.broadcasted_iota(jnp.int32, values.shape, 0)
    return jnp.where(rows < populations, values, 0.0)


def pad_rows(values, rows):
    spare = jnp.zeros((rows - values.shape[0], values.shape[1]), values.dtype)
    return jnp.concatenate([values, spare], axis=0)


def put_packed(ref, first, stride, values):
    count = values.shape[0]
    for block in range(values.shape[1] // LANES):
        top = block * stride + first
        ref[top : top + count, :] = values[:, block * LANES : (block + 1) * LANES]


def sum_packed(parts, first, stride, count):
    pieces = []
    for top in range(first, parts[0].shape[0], stride):
        here = slice(top, top + count)
        pieces.append(pair_sum([part[here, :] for part in parts]))
    return jnp.concatenate(pieces, axis=1)


def variant_sums(
    populations, mixture, alleles, alt_ref, ref_ref, both_ref, gap_high, gap_low, turned
):
    rows, samples = mixture.shape
    variants = alleles.shape[1]
    tall, wide = blocks_of(samples, TALL), blocks_of(variants, WIDE)
    mix_high, mix_mid, mix_low = split(mixture)
    all_high, all_mid, all_low = split(alleles)
    turned[...] = jnp.concatenate(
        [mix_high, mix_high, mix_mid, mix_mid, mix_high, mix_low], axis=0
    ).T
    right = jnp.concatenate([all_high, all_mid, all_high, all_mid, all_low, all_high], axis=0)
    left = jnp.concatenate([mix_high, mix_mid], axis=0)
    for start in range(0, variants, wide):
        across = slice(start, start + wide)
        excess = jnp.zeros((2 * rows, wide), F32)
        ref_sum = jnp.zeros((2 * rows, wide), F32)
        for top in range(0, samples, tall):
            here = slice(top, top + tall)
            expected = dot(turned[here, :], right[:, across], 1, 0)
            ref = ref_ref[here, across] * pl.reciprocal(1.0 - expected, approx=True)
            gap = alt_ref[here, across] * pl.reciprocal(expected, approx=True) - ref
            for table, term in zip((gap_high, gap_low), two_terms(gap)):
                table[here, across] = term
                excess = excess + dot(left[:, here], term, 1, 0)
            for term in two_terms(ref):
                ref_sum = ref_sum + dot(left[:, here], term, 1, 0)
        excess = excess[:populations] + excess[rows : rows + populations]
        ref_sum = ref_sum[:populations] + ref_sum[rows : rows + populations]
        first_block = start // LANES * 2 * populations
        put_packed(both_ref, first_block, 2 * populations, excess + ref_sum)
        put_packed(both_ref, first_block + populations, 2 * populations, ref_sum)


def sample_sums_kernel(populations, mixture, alleles, twice_here, gap_high, gap_low, prop_ref):
    samples = mixture.shape[1]
    rows = alleles.shape[0]
    all_high, all_mid, _ = split(alleles[...])
    toward = jnp.concatenate([all_high, all_mid], axis=0)
    prop = dot(toward, gap_high[...], 1, 1) + dot(toward, gap_low[...], 1, 1)
    prop = prop[:populations] + prop[rows : rows + populations]
    along = jnp.sum(mixture[:populations, :] * prop, axis=0, keepdims=True)
    stride = prop_ref.shape[0] * LANES // samples
    put_packed(prop_ref, 0, stride, prop + (twice_here[...] - along))
    if stride > populations:
        put_packed(prop_ref, populations, stride, twice_here[...])


def next_mixture(populations, mixture, twice_observed, prop_parts):
    rows, samples = mixture.shape
    stride = prop_parts[0].shape[0] * LANES // samples
    prop_sums = sum_packed(prop_parts, 0, stride, populations)
    if twice_observed is None:
        twice_observed = sum_packed(prop_parts, populations, stride, 1)
    moved = clip_unit(mixture[:populations] * prop_sums / twice_observed)
    return pad_rows(moved, rows), twice_observed


def next_alleles(populations, alleles, both_parts):
    alt_sums = sum_packed(both_parts, 0, 2 * populations, populations)
    ref_sums = sum_packed(both_parts, populations, 2 * populations, populations)
    current = alleles[:populations]
    weighted = current * alt_sums
    moved = clip_unit(weighted / (weighted + (1.0 - current) * ref_sums))
    return pad_rows(moved, alleles.shape[0])


def prepare_kernel(genotypes, observed, alt_out, ref_out, twice_out, landed, arrivals):
    samples, variants = genotypes.shape
    tall = samples // arrivals.shape[1]
    copies = []
    for index, top in enumerate(range(0, samples, tall)):
        here = pl.ds(top, tall)
        for place, source in enumerate((genotypes, observed)):
            copy = pltpu.make_async_copy(
                source.at[here, :], landed.at[place, here, :], arrivals.at[place, index]
            )
            copy.start()
            copies.append(copy)
    ones = jnp.ones((SUBLANES, variants), BF16)
    for index, top in enumerate(range(0, samples, tall)):
        here = slice(top, top + tall)
        copies[2 * index].wait()
        copies[2 * index + 1].wait()
        seen = landed[1, here, :].astype(F32)
        alt = seen * landed[0, here, :].astype(F32)
        alt_out[here, :] = alt
        ref_out[here, :] = 2.0 * seen - alt
        twice_out[:, here] = 2.0 * dot(ones, seen.astype(BF16), 1, 1)[:1]


def first_kernel(mixture, alleles, alt, ref, mixture_out, alleles_out, both_out, *refs):
    populations = mixture.shape[0]
    rows = mixture_out.shape[0]
    mix = pad_rows(mixture[...], rows)
    current = pad_rows(alleles[...], rows)
    mixture_out[...] = mix
    alleles_out[...] = current
    variant_sums(populations, mix, current, alt, ref, both_out, *refs)


def mixture_kernel(populations, with_twice, mixture, *refs):
    twice = refs[0][...] if with_twice else None
    prop_parts, outs = split_refs(refs[with_twice:], len(refs) - 2)
    mix, twice = next_mixture(populations, mixture[...], twice, prop_parts)
    outs[0][...] = mix
    if not with_twice:
        outs[1][...] = twice


def step_kernel(populations, mixture, alleles, *refs):
    both_parts, (alt, ref, alleles_out, both_out), refs = split_refs(refs, 2, 4)
    current = next_alleles(populations, alleles[...], both_parts)
    alleles_out[...] = current
    variant_sums(populations, mixture[...], current, alt, ref, both_out, *refs)


def split_refs(refs, *counts):
    groups = []
    for count in counts:
        groups.append(refs[:count])
        refs = refs[count:]
    return (*groups, refs)


def folded(values):
    squares = values * values
    tile = squares.reshape(-1, SUBLANES, squares.shape[1]).sum(axis=0)
    width = tile.shape[1]
    return sum(tile[:, i : i + LANES] for i in range(0, width, LANES))


def squares(zero, one, two, tile):
    step = one - zero
    tile[:SUBLANES, :] = folded(step)
    tile[SUBLANES:, :] = folded(two - one - step)


def mixture_square_kernel(populations, zero, one, twice, *refs):
    prop_parts, (two_out, tile) = split_refs(refs, len(refs) - 2)
    two, _ = next_mixture(populations, one[...], twice[...], prop_parts)
    two_out[...] = two
    squares(zero[...], one[...], two, tile)


def alleles_square_kernel(populations, zero, one, *refs):
    both_parts, (two_out, tile) = split_refs(refs, 2)
    two = next_alleles(populations, one[...], both_parts)
    two_out[...] = two
    squares(zero[...], one[...], two, tile)


def leap(zero, one, two, tile):
    first = jnp.sum(tile[:SUBLANES], axis=(0, 1), keepdims=True)
    second = jnp.sum(tile[SUBLANES:], axis=(0, 1), keepdims=True)
    alpha = jnp.maximum(1.0, jnp.sqrt(first / (second + NORM_EPS)))
    step = one - zero
    curve = two - one - step
    return zero + 2.0 * alpha * step + alpha * alpha * curve


def leap_kernel(populations, *refs):
    states = [ref[...] for ref in refs[:6]]
    mix_zero, all_zero, mix_one, all_one, mix_two, all_two = states
    mix_parts, all_parts, rest = split_refs(refs[6:], 2, 2)
    alt, ref, mixture_out, alleles_out, both_out, *refs = rest
    mix_tile = mix_parts[0][...] + mix_parts[1][...]
    all_tile = all_parts[0][...] + all_parts[1][...]
    clipped = row_mask(clip_unit(leap(mix_zero, mix_one, mix_two, mix_tile)), populations)
    mix = clipped / jnp.sum(clipped, axis=0, keepdims=True)
    current = row_mask(clip_unit(leap(all_zero, all_one, all_two, all_tile)), populations)
    mixture_out[...] = mix
    alleles_out[...] = current
    variant_sums(populations, mix, current, alt, ref, both_out, *refs)


def last_kernel(populations, mixture, alleles, *refs):
    both_parts, (mixture_out, alleles_out) = split_refs(refs, 2)
    mixture_out[...] = mixture[:populations, :]
    alleles_out[...] = next_alleles(populations, alleles[...], both_parts)[:populations]


def call(kernel, name, outs, args, scratch=(), flops=0):
    whole = pl.BlockSpec(memory_space=pltpu.VMEM)
    cost = pl.CostEstimate(flops=flops, bytes_accessed=0, transcendentals=0) if flops else None
    return pl.pallas_call(
        kernel,
        out_shape=tuple(jax.ShapeDtypeStruct(*out) for out in outs),
        in_specs=[pl.BlockSpec(memory_space=pltpu.VMEM)] * len(args),
        out_specs=(whole,) * len(outs),
        scratch_shapes=list(scratch),
        compiler_params=pltpu.CompilerParams(vmem_limit_bytes=VMEM_BYTES),
        cost_estimate=cost,
        name=name,
    )(*args)


def local(genotypes, observed, proportions, frequencies):
    populations, samples = proportions.shape
    variants = genotypes.shape[1]
    rows = -(-populations // 16) * 16
    state_out = (((rows, samples), F32), ((rows, variants), F32))
    packed = populations * samples // LANES
    both_out = ((2 * populations * variants // LANES, LANES), F32)
    sums_out = (both_out, ((samples, variants), BF16), ((samples, variants), BF16))
    tile_out = ((2 * SUBLANES, LANES), F32)
    turned = (pltpu.VMEM((samples, 6 * rows), BF16),)

    chunks = samples // blocks_of(samples, 128)
    flags, genotypes, observed = lax.optimization_barrier((gather_flags(), genotypes, observed))
    in_place = [
        pltpu.with_memory_space_constraint(array, pltpu.HBM) for array in (genotypes, observed)
    ]
    whole = pl.BlockSpec(memory_space=pltpu.VMEM)
    alt, ref, twice_here = pl.pallas_call(
        prepare_kernel,
        out_shape=(
            pltpu.VMEM((samples, variants), F32),
            pltpu.VMEM((samples, variants), F32),
            jax.ShapeDtypeStruct((1, samples), F32),
        ),
        in_specs=[pl.BlockSpec(memory_space=pltpu.HBM)] * 2,
        out_specs=(whole,) * 3,
        scratch_shapes=[
            pltpu.VMEM((2, samples, variants), jnp.int32),
            pltpu.SemaphoreType.DMA((2, chunks)),
        ],
        compiler_params=pltpu.CompilerParams(vmem_limit_bytes=VMEM_BYTES),
        name="prepare",
    )(*in_place)
    alleles = gather_frequencies(frequencies, flags)

    def sums(mixture, alleles, both, gaps, extra=0):
        (prop,) = call(
            functools.partial(sample_sums_kernel, populations),
            "sample_sums",
            (((packed + extra, LANES), F32),),
            (mixture, alleles, twice_here, *gaps),
        )
        both = both + swap(both, "samp", 1)
        return lax.optimization_barrier((prop, both))

    mix_zero, all_zero, both, *gaps = call(
        first_kernel,
        "first",
        (*state_out, *sums_out),
        (proportions, alleles, alt, ref),
        turned,
    )
    prop, both = sums(mix_zero, all_zero, both, gaps, samples // LANES)

    def moved_mixture(mixture, twice, prop):
        known = () if twice is None else (twice,)
        extra = () if known else (((1, samples), F32),)
        out = call(
            functools.partial(mixture_kernel, populations, len(known)),
            "mixture",
            (state_out[0], *extra),
            (mixture, *known, *all_parts_of(prop, "var")),
            flops=MIXTURE_COST,
        )
        return out[0], (known or out[1:])[0]

    def step(mixture, alleles, both):
        moved, both, *gaps = call(
            functools.partial(step_kernel, populations),
            "step",
            (state_out[1], *sums_out),
            (mixture, alleles, *parts_of(both, "samp", 1), alt, ref),
            turned,
        )
        return moved, *sums(mixture, moved, both, gaps)

    twice = None
    for repeat in range(STEPS):
        if repeat:
            mix_zero, twice = moved_mixture(mix_zero, twice, prop)
            all_zero, prop, both = step(mix_zero, all_zero, both)
        mix_one, twice = moved_mixture(mix_zero, twice, prop)
        all_one, prop, both = step(mix_one, all_zero, both)
        mix_two, mix_tile = call(
            functools.partial(mixture_square_kernel, populations),
            "mixture_square",
            (state_out[0], tile_out),
            (mix_zero, mix_one, twice, *all_parts_of(prop, "var")),
            flops=MIXTURE_COST,
        )
        all_two, all_tile = call(
            functools.partial(alleles_square_kernel, populations),
            "alleles_square",
            (state_out[1], tile_out),
            (all_zero, all_one, *parts_of(both, "samp", 1)),
            flops=ALLELES_COST,
        )
        mix_tile = mix_tile + swap(mix_tile, "samp", 1)
        tiles = (*parts_of(mix_tile, "samp", 1), *parts_of(all_tile, "var"))
        mix_zero, all_zero, both, *gaps = call(
            functools.partial(leap_kernel, populations),
            "leap",
            (*state_out, *sums_out),
            (mix_zero, all_zero, mix_one, all_one, mix_two, all_two, *tiles, alt, ref),
            turned,
        )
        prop, both = sums(mix_zero, all_zero, both, gaps)
    mixture, _ = moved_mixture(mix_zero, twice, prop)
    return call(
        functools.partial(last_kernel, populations),
        "last",
        (((populations, samples), F32), ((populations, variants), F32)),
        (mixture, all_zero, *parts_of(both, "samp", 1)),
    )


def solution(mesh):
    placed = (P("samp", "var"), P("samp", "var"), P(None, "samp"), P(None, ("samp", "var")))
    return jax.shard_map(
        local,
        mesh=mesh,
        in_specs=placed,
        out_specs=(P(None, "samp"), P(None, "var")),
        check_vma=False,
    )
```

```python
import functools

import jax
import jax.numpy as jnp
from jax import lax
from jax.experimental import pallas as pl
from jax.experimental.pallas import tpu as pltpu
from jax.sharding import PartitionSpec as P

STEPS = 2
CLIP_LOW = 1e-05
NORM_EPS = 1e-10
F32 = jnp.float32
BF16 = jnp.bfloat16
SUBLANES = 8
LANES = 128
VMEM_BYTES = 32 * 2**20
TALL, WIDE = 512, 1024
MIXTURE_COST = 5 * 10**9
ALLELES_COST = 5 * 10**9


def clip_unit(values):
    return jnp.clip(values, CLIP_LOW, 1.0 - CLIP_LOW)


def blocks_of(size, largest):
    width = min(size, largest)
    while size % width:
        width -= 1
    return width


def swap(value, axis, mask):
    size = lax.axis_size(axis)
    return lax.ppermute(value, axis, [(i, i ^ mask) for i in range(size)])


def strides_of(axis):
    return [1 << bit for bit in range(lax.axis_size(axis).bit_length() - 1)]


def all_parts_of(value, axis):
    return [value] + [swap(value, axis, i ^ (i >> 1)) for i in range(1, lax.axis_size(axis))]


def pair_sum(parts):
    while len(parts) > 1:
        parts = [a + b for a, b in zip(parts[::2], parts[1::2])]
    return parts[0]


def parts_of(value, axis, done=0):
    strides = strides_of(axis)[done:]
    for stride in strides[:-1]:
        value = value + swap(value, axis, stride)
    return value, swap(value, axis, strides[-1])


def gather_flags():
    samp_count, var_count = lax.axis_size("samp"), lax.axis_size("var")
    group = samp_count // var_count
    samp, var = lax.axis_index("samp"), lax.axis_index("var")
    var_bits = [(var & stride) != 0 for stride in strides_of("var")]
    samp_bits = [(samp & stride) != 0 for stride in strides_of("samp") if stride < group]
    return samp // group == var, var_bits, samp_bits


def gather_frequencies(frequencies, flags):
    owns, var_bits, samp_bits = flags
    samp_count, var_count = lax.axis_size("samp"), lax.axis_size("var")
    group = samp_count // var_count
    both = ("samp", "var")
    arrived = []
    for mask in range(1, var_count):
        pairs = [
            (s * var_count + ((s // group) ^ mask), s * var_count + s // group)
            for s in range(samp_count)
        ]
        arrived.append(lax.ppermute(frequencies, both, pairs))
    arrived = [jnp.where(owns, frequencies, 0.0)] + arrived
    for bit, flip in enumerate(var_bits):
        arrived = [jnp.where(flip, arrived[i ^ (1 << bit)], arrived[i]) for i in range(var_count)]
    held = jnp.concatenate(arrived, axis=1)
    for bit, upper in enumerate(samp_bits):
        other = swap(held, "samp", 1 << bit)
        held = jnp.concatenate(
            [jnp.where(upper, other, held), jnp.where(upper, held, other)], axis=1
        )
    held = jnp.where(owns, held, 0.0)
    total = held
    for mask in range(1, var_count):
        pairs = [
            ((v * group + g) * var_count + v, ((v ^ mask) * group + g) * var_count + v)
            for v in range(var_count)
            for g in range(group)
        ]
        total = total + lax.ppermute(held, both, pairs)
    return total


def dot(left, right, left_dim, right_dim):
    return lax.dot_general(
        left, right, (((left_dim,), (right_dim,)), ((), ())), preferred_element_type=F32
    )


def split(values):
    high = values.astype(BF16)
    rest = values - high.astype(F32)
    middle = rest.astype(BF16)
    return high, middle, (rest - middle.astype(F32)).astype(BF16)


def two_terms(values):
    high = values.astype(BF16)
    return high, (values - high.astype(F32)).astype(BF16)


def row_mask(values, populations):
    rows = lax.broadcasted_iota(jnp.int32, values.shape, 0)
    return jnp.where(rows < populations, values, 0.0)


def pad_rows(values, rows):
    spare = jnp.zeros((rows - values.shape[0], values.shape[1]), values.dtype)
    return jnp.concatenate([values, spare], axis=0)


def put_packed(ref, first, stride, values):
    count = values.shape[0]
    for block in range(values.shape[1] // LANES):
        top = block * stride + first
        ref[top : top + count, :] = values[:, block * LANES : (block + 1) * LANES]


def sum_packed(parts, first, stride, count):
    pieces = []
    for top in range(first, parts[0].shape[0], stride):
        here = slice(top, top + count)
        pieces.append(pair_sum([part[here, :] for part in parts]))
    return jnp.concatenate(pieces, axis=1)


def variant_sums(
    populations, mixture, alleles, alt_ref, ref_ref, both_ref, gap_high, gap_low, turned
):
    rows, samples = mixture.shape
    variants = alleles.shape[1]
    tall, wide = blocks_of(samples, TALL), blocks_of(variants, WIDE)
    mix_high, mix_mid, mix_low = split(mixture)
    all_high, all_mid, all_low = split(alleles)
    turned[...] = jnp.concatenate(
        [mix_high, mix_high, mix_mid, mix_mid, mix_high, mix_low], axis=0
    ).T
    right = jnp.concatenate([all_high, all_mid, all_high, all_mid, all_low, all_high], axis=0)
    left = jnp.concatenate([mix_high, mix_mid], axis=0)
    for start in range(0, variants, wide):
        across = slice(start, start + wide)
        excess = jnp.zeros((2 * rows, wide), F32)
        ref_sum = jnp.zeros((2 * rows, wide), F32)
        for top in range(0, samples, tall):
            here = slice(top, top + tall)
            expected = dot(turned[here, :], right[:, across], 1, 0)
            ref = ref_ref[here, across] * pl.reciprocal(1.0 - expected, approx=True)
            gap = alt_ref[here, across] * pl.reciprocal(expected, approx=True) - ref
            for table, term in zip((gap_high, gap_low), two_terms(gap)):
                table[here, across] = term
                excess = excess + dot(left[:, here], term, 1, 0)
            for term in two_terms(ref):
                ref_sum = ref_sum + dot(left[:, here], term, 1, 0)
        excess = excess[:populations] + excess[rows : rows + populations]
        ref_sum = ref_sum[:populations] + ref_sum[rows : rows + populations]
        first_block = start // LANES * 2 * populations
        put_packed(both_ref, first_block, 2 * populations, excess + ref_sum)
        put_packed(both_ref, first_block + populations, 2 * populations, ref_sum)


def sample_sums_kernel(populations, mixture, alleles, twice_here, gap_high, gap_low, prop_ref):
    samples = mixture.shape[1]
    rows = alleles.shape[0]
    all_high, all_mid, _ = split(alleles[...])
    toward = jnp.concatenate([all_high, all_mid], axis=0)
    prop = dot(toward, gap_high[...], 1, 1) + dot(toward, gap_low[...], 1, 1)
    prop = prop[:populations] + prop[rows : rows + populations]
    along = jnp.sum(mixture[:populations, :] * prop, axis=0, keepdims=True)
    stride = prop_ref.shape[0] * LANES // samples
    put_packed(prop_ref, 0, stride, prop + (twice_here[...] - along))
    if stride > populations:
        put_packed(prop_ref, populations, stride, twice_here[...])


def next_mixture(populations, mixture, twice_observed, prop_parts):
    rows, samples = mixture.shape
    stride = prop_parts[0].shape[0] * LANES // samples
    prop_sums = sum_packed(prop_parts, 0, stride, populations)
    if twice_observed is None:
        twice_observed = sum_packed(prop_parts, populations, stride, 1)
    moved = clip_unit(mixture[:populations] * prop_sums / twice_observed)
    return pad_rows(moved, rows), twice_observed


def next_alleles(populations, alleles, both_parts):
    alt_sums = sum_packed(both_parts, 0, 2 * populations, populations)
    ref_sums = sum_packed(both_parts, populations, 2 * populations, populations)
    current = alleles[:populations]
    weighted = current * alt_sums
    moved = clip_unit(weighted / (weighted + (1.0 - current) * ref_sums))
    return pad_rows(moved, alleles.shape[0])


def prepare_kernel(genotypes, observed, alt_out, ref_out, twice_out, landed, arrivals):
    samples, variants = genotypes.shape
    tall = samples // arrivals.shape[1]
    copies = []
    for index, top in enumerate(range(0, samples, tall)):
        here = pl.ds(top, tall)
        for place, source in enumerate((genotypes, observed)):
            copy = pltpu.make_async_copy(
                source.at[here, :], landed.at[place, here, :], arrivals.at[place, index]
            )
            copy.start()
            copies.append(copy)
    ones = jnp.ones((SUBLANES, variants), BF16)
    for index, top in enumerate(range(0, samples, tall)):
        here = slice(top, top + tall)
        copies[2 * index].wait()
        copies[2 * index + 1].wait()
        seen = landed[1, here, :].astype(F32)
        alt = seen * landed[0, here, :].astype(F32)
        alt_out[here, :] = alt
        ref_out[here, :] = 2.0 * seen - alt
        twice_out[:, here] = 2.0 * dot(ones, seen.astype(BF16), 1, 1)[:1]


def first_kernel(mixture, alleles, alt, ref, mixture_out, alleles_out, both_out, *refs):
    populations = mixture.shape[0]
    rows = mixture_out.shape[0]
    mix = pad_rows(mixture[...], rows)
    current = pad_rows(alleles[...], rows)
    mixture_out[...] = mix
    alleles_out[...] = current
    variant_sums(populations, mix, current, alt, ref, both_out, *refs)


def mixture_kernel(populations, with_twice, mixture, *refs):
    twice = refs[0][...] if with_twice else None
    prop_parts, outs = split_refs(refs[with_twice:], len(refs) - 2)
    mix, twice = next_mixture(populations, mixture[...], twice, prop_parts)
    outs[0][...] = mix
    if not with_twice:
        outs[1][...] = twice


def step_kernel(populations, mixture, alleles, *refs):
    both_parts, (alt, ref, alleles_out, both_out), refs = split_refs(refs, 2, 4)
    current = next_alleles(populations, alleles[...], both_parts)
    alleles_out[...] = current
    variant_sums(populations, mixture[...], current, alt, ref, both_out, *refs)


def split_refs(refs, *counts):
    groups = []
    for count in counts:
        groups.append(refs[:count])
        refs = refs[count:]
    return (*groups, refs)


def folded(values):
    squares = values * values
    tile = squares.reshape(-1, SUBLANES, squares.shape[1]).sum(axis=0)
    width = tile.shape[1]
    return sum(tile[:, i : i + LANES] for i in range(0, width, LANES))


def squares(zero, one, two, tile):
    step = one - zero
    tile[:SUBLANES, :] = folded(step)
    tile[SUBLANES:, :] = folded(two - one - step)


def mixture_square_kernel(populations, zero, one, twice, *refs):
    prop_parts, (two_out, tile) = split_refs(refs, len(refs) - 2)
    two, _ = next_mixture(populations, one[...], twice[...], prop_parts)
    two_out[...] = two
    squares(zero[...], one[...], two, tile)


def alleles_square_kernel(populations, zero, one, *refs):
    both_parts, (two_out, tile) = split_refs(refs, 2)
    two = next_alleles(populations, one[...], both_parts)
    two_out[...] = two
    squares(zero[...], one[...], two, tile)


def leap(zero, one, two, tile):
    first = jnp.sum(tile[:SUBLANES], axis=(0, 1), keepdims=True)
    second = jnp.sum(tile[SUBLANES:], axis=(0, 1), keepdims=True)
    alpha = jnp.maximum(1.0, jnp.sqrt(first / (second + NORM_EPS)))
    step = one - zero
    curve = two - one - step
    return zero + 2.0 * alpha * step + alpha * alpha * curve


def leap_kernel(populations, n_all, *refs):
    states = [ref[...] for ref in refs[:6]]
    mix_zero, all_zero, mix_one, all_one, mix_two, all_two = states
    mix_parts, all_parts, rest = split_refs(refs[6:], 2, n_all)
    alt, ref, mixture_out, alleles_out, both_out, *refs = rest
    mix_tile = mix_parts[0][...] + mix_parts[1][...]
    all_tile = pair_sum([part[...] for part in all_parts])
    clipped = row_mask(clip_unit(leap(mix_zero, mix_one, mix_two, mix_tile)), populations)
    mix = clipped / jnp.sum(clipped, axis=0, keepdims=True)
    current = row_mask(clip_unit(leap(all_zero, all_one, all_two, all_tile)), populations)
    mixture_out[...] = mix
    alleles_out[...] = current
    variant_sums(populations, mix, current, alt, ref, both_out, *refs)


def last_kernel(populations, mixture, alleles, *refs):
    both_parts, (mixture_out, alleles_out) = split_refs(refs, 2)
    mixture_out[...] = mixture[:populations, :]
    alleles_out[...] = next_alleles(populations, alleles[...], both_parts)[:populations]


def call(kernel, name, outs, args, scratch=(), flops=0):
    whole = pl.BlockSpec(memory_space=pltpu.VMEM)
    cost = pl.CostEstimate(flops=flops, bytes_accessed=0, transcendentals=0) if flops else None
    return pl.pallas_call(
        kernel,
        out_shape=tuple(jax.ShapeDtypeStruct(*out) for out in outs),
        in_specs=[pl.BlockSpec(memory_space=pltpu.VMEM)] * len(args),
        out_specs=(whole,) * len(outs),
        scratch_shapes=list(scratch),
        compiler_params=pltpu.CompilerParams(vmem_limit_bytes=VMEM_BYTES),
        cost_estimate=cost,
        name=name,
    )(*args)


def local(genotypes, observed, proportions, frequencies):
    populations, samples = proportions.shape
    variants = genotypes.shape[1]
    rows = -(-populations // 16) * 16
    state_out = (((rows, samples), F32), ((rows, variants), F32))
    packed = populations * samples // LANES
    both_out = ((2 * populations * variants // LANES, LANES), F32)
    sums_out = (both_out, ((samples, variants), BF16), ((samples, variants), BF16))
    tile_out = ((2 * SUBLANES, LANES), F32)
    turned = (pltpu.VMEM((samples, 6 * rows), BF16),)

    chunks = samples // blocks_of(samples, 128)
    flags, genotypes, observed = lax.optimization_barrier((gather_flags(), genotypes, observed))
    in_place = [
        pltpu.with_memory_space_constraint(array, pltpu.HBM) for array in (genotypes, observed)
    ]
    whole = pl.BlockSpec(memory_space=pltpu.VMEM)
    alt, ref, twice_here = pl.pallas_call(
        prepare_kernel,
        out_shape=(
            pltpu.VMEM((samples, variants), F32),
            pltpu.VMEM((samples, variants), F32),
            jax.ShapeDtypeStruct((1, samples), F32),
        ),
        in_specs=[pl.BlockSpec(memory_space=pltpu.HBM)] * 2,
        out_specs=(whole,) * 3,
        scratch_shapes=[
            pltpu.VMEM((2, samples, variants), jnp.int32),
            pltpu.SemaphoreType.DMA((2, chunks)),
        ],
        compiler_params=pltpu.CompilerParams(vmem_limit_bytes=VMEM_BYTES),
        name="prepare",
    )(*in_place)
    alleles = gather_frequencies(frequencies, flags)

    def sums(mixture, alleles, both, gaps, extra=0):
        (prop,) = call(
            functools.partial(sample_sums_kernel, populations),
            "sample_sums",
            (((packed + extra, LANES), F32),),
            (mixture, alleles, twice_here, *gaps),
        )
        both = both + swap(both, "samp", 1)
        return lax.optimization_barrier((prop, both))

    mix_zero, all_zero, both, *gaps = call(
        first_kernel,
        "first",
        (*state_out, *sums_out),
        (proportions, alleles, alt, ref),
        turned,
    )
    prop, both = sums(mix_zero, all_zero, both, gaps, samples // LANES)

    def moved_mixture(mixture, twice, prop):
        known = () if twice is None else (twice,)
        extra = () if known else (((1, samples), F32),)
        out = call(
            functools.partial(mixture_kernel, populations, len(known)),
            "mixture",
            (state_out[0], *extra),
            (mixture, *known, *all_parts_of(prop, "var")),
            flops=MIXTURE_COST,
        )
        return out[0], (known or out[1:])[0]

    def step(mixture, alleles, both):
        moved, both, *gaps = call(
            functools.partial(step_kernel, populations),
            "step",
            (state_out[1], *sums_out),
            (mixture, alleles, *parts_of(both, "samp", 1), alt, ref),
            turned,
        )
        return moved, *sums(mixture, moved, both, gaps)

    twice = None
    for repeat in range(STEPS):
        if repeat:
            mix_zero, twice = moved_mixture(mix_zero, twice, prop)
            all_zero, prop, both = step(mix_zero, all_zero, both)
        mix_one, twice = moved_mixture(mix_zero, twice, prop)
        all_one, prop, both = step(mix_one, all_zero, both)
        mix_two, mix_tile = call(
            functools.partial(mixture_square_kernel, populations),
            "mixture_square",
            (state_out[0], tile_out),
            (mix_zero, mix_one, twice, *all_parts_of(prop, "var")),
            flops=MIXTURE_COST,
        )
        all_two, all_tile = call(
            functools.partial(alleles_square_kernel, populations),
            "alleles_square",
            (state_out[1], tile_out),
            (all_zero, all_one, *parts_of(both, "samp", 1)),
            flops=ALLELES_COST,
        )
        mix_tile = mix_tile + swap(mix_tile, "samp", 1)
        mix_tile, all_tile = lax.optimization_barrier((mix_tile, all_tile))
        tiles = (*parts_of(mix_tile, "samp", 1), *all_parts_of(all_tile, "var"))
        mix_zero, all_zero, both, *gaps = call(
            functools.partial(leap_kernel, populations, len(tiles) - 2),
            "leap",
            (*state_out, *sums_out),
            (mix_zero, all_zero, mix_one, all_one, mix_two, all_two, *tiles, alt, ref),
            turned,
        )
        prop, both = sums(mix_zero, all_zero, both, gaps)
    mixture, _ = moved_mixture(mix_zero, twice, prop)
    return call(
        functools.partial(last_kernel, populations),
        "last",
        (((populations, samples), F32), ((populations, variants), F32)),
        (mixture, all_zero, *parts_of(both, "samp", 1)),
    )


def solution(mesh):
    placed = (P("samp", "var"), P("samp", "var"), P(None, "samp"), P(None, ("samp", "var")))
    return jax.shard_map(
        local,
        mesh=mesh,
        in_specs=placed,
        out_specs=(P(None, "samp"), P(None, "var")),
        check_vma=False,
    )
```

```python
import functools

import jax
import jax.numpy as jnp
from jax import lax
from jax.experimental import pallas as pl
from jax.experimental.pallas import tpu as pltpu
from jax.sharding import PartitionSpec as P

STEPS = 2
CLIP_LOW = 1e-05
NORM_EPS = 1e-10
F32 = jnp.float32
BF16 = jnp.bfloat16
SUBLANES = 8
LANES = 128
VMEM_BYTES = 32 * 2**20
TALL, WIDE = 1024, 1024
MIXTURE_COST = 5 * 10**9
ALLELES_COST = 5 * 10**9


def clip_unit(values):
    return jnp.clip(values, CLIP_LOW, 1.0 - CLIP_LOW)


def blocks_of(size, largest):
    width = min(size, largest)
    while size % width:
        width -= 1
    return width


def swap(value, axis, mask):
    size = lax.axis_size(axis)
    return lax.ppermute(value, axis, [(i, i ^ mask) for i in range(size)])


def strides_of(axis):
    return [1 << bit for bit in range(lax.axis_size(axis).bit_length() - 1)]


def all_parts_of(value, axis):
    return [value] + [swap(value, axis, i ^ (i >> 1)) for i in range(1, lax.axis_size(axis))]


def pair_sum(parts):
    while len(parts) > 1:
        parts = [a + b for a, b in zip(parts[::2], parts[1::2])]
    return parts[0]


def parts_of(value, axis, done=0):
    strides = strides_of(axis)[done:]
    for stride in strides[:-1]:
        value = value + swap(value, axis, stride)
    return value, swap(value, axis, strides[-1])


def gather_flags():
    samp_count, var_count = lax.axis_size("samp"), lax.axis_size("var")
    group = samp_count // var_count
    samp, var = lax.axis_index("samp"), lax.axis_index("var")
    var_bits = [(var & stride) != 0 for stride in strides_of("var")]
    samp_bits = [(samp & stride) != 0 for stride in strides_of("samp") if stride < group]
    return samp // group == var, var_bits, samp_bits


def gather_frequencies(frequencies, flags):
    owns, var_bits, samp_bits = flags
    samp_count, var_count = lax.axis_size("samp"), lax.axis_size("var")
    group = samp_count // var_count
    both = ("samp", "var")
    arrived = []
    for mask in range(1, var_count):
        pairs = [
            (s * var_count + ((s // group) ^ mask), s * var_count + s // group)
            for s in range(samp_count)
        ]
        arrived.append(lax.ppermute(frequencies, both, pairs))
    arrived = [jnp.where(owns, frequencies, 0.0)] + arrived
    for bit, flip in enumerate(var_bits):
        arrived = [jnp.where(flip, arrived[i ^ (1 << bit)], arrived[i]) for i in range(var_count)]
    held = jnp.concatenate(arrived, axis=1)
    for bit, upper in enumerate(samp_bits):
        other = swap(held, "samp", 1 << bit)
        held = jnp.concatenate(
            [jnp.where(upper, other, held), jnp.where(upper, held, other)], axis=1
        )
    held = jnp.where(owns, held, 0.0)
    total = held
    for mask in range(1, var_count):
        pairs = [
            ((v * group + g) * var_count + v, ((v ^ mask) * group + g) * var_count + v)
            for v in range(var_count)
            for g in range(group)
        ]
        total = total + lax.ppermute(held, both, pairs)
    return total


def dot(left, right, left_dim, right_dim):
    return lax.dot_general(
        left, right, (((left_dim,), (right_dim,)), ((), ())), preferred_element_type=F32
    )


def split(values):
    high = values.astype(BF16)
    rest = values - high.astype(F32)
    middle = rest.astype(BF16)
    return high, middle, (rest - middle.astype(F32)).astype(BF16)


def two_terms(values):
    high = values.astype(BF16)
    return high, (values - high.astype(F32)).astype(BF16)


def row_mask(values, populations):
    rows = lax.broadcasted_iota(jnp.int32, values.shape, 0)
    return jnp.where(rows < populations, values, 0.0)


def pad_rows(values, rows):
    spare = jnp.zeros((rows - values.shape[0], values.shape[1]), values.dtype)
    return jnp.concatenate([values, spare], axis=0)


def put_packed(ref, first, stride, values):
    count = values.shape[0]
    for block in range(values.shape[1] // LANES):
        top = block * stride + first
        ref[top : top + count, :] = values[:, block * LANES : (block + 1) * LANES]


def sum_packed(parts, first, stride, count):
    pieces = []
    for top in range(first, parts[0].shape[0], stride):
        here = slice(top, top + count)
        pieces.append(pair_sum([part[here, :] for part in parts]))
    return jnp.concatenate(pieces, axis=1)


def variant_sums(
    populations, mixture, alleles, alt_ref, ref_ref, both_ref, gap_high, gap_low, turned
):
    rows, samples = mixture.shape
    variants = alleles.shape[1]
    tall, wide = blocks_of(samples, TALL), blocks_of(variants, WIDE)
    mix_high, mix_mid, mix_low = split(mixture)
    all_high, all_mid, all_low = split(alleles)
    turned[...] = jnp.concatenate(
        [mix_high, mix_high, mix_mid, mix_mid, mix_high, mix_low], axis=0
    ).T
    right = jnp.concatenate([all_high, all_mid, all_high, all_mid, all_low, all_high], axis=0)
    left = jnp.concatenate([mix_high, mix_mid], axis=0)
    for start in range(0, variants, wide):
        across = slice(start, start + wide)
        excess = jnp.zeros((2 * rows, wide), F32)
        ref_sum = jnp.zeros((2 * rows, wide), F32)
        for top in range(0, samples, tall):
            here = slice(top, top + tall)
            expected = dot(turned[here, :], right[:, across], 1, 0)
            ref = ref_ref[here, across] * pl.reciprocal(1.0 - expected, approx=True)
            gap = alt_ref[here, across] * pl.reciprocal(expected, approx=True) - ref
            for table, term in zip((gap_high, gap_low), two_terms(gap)):
                table[here, across] = term
                excess = excess + dot(left[:, here], term, 1, 0)
            for term in two_terms(ref):
                ref_sum = ref_sum + dot(left[:, here], term, 1, 0)
        excess = excess[:populations] + excess[rows : rows + populations]
        ref_sum = ref_sum[:populations] + ref_sum[rows : rows + populations]
        first_block = start // LANES * 2 * populations
        put_packed(both_ref, first_block, 2 * populations, excess + ref_sum)
        put_packed(both_ref, first_block + populations, 2 * populations, ref_sum)


def sample_sums_kernel(populations, mixture, alleles, twice_here, gap_high, gap_low, prop_ref):
    samples = mixture.shape[1]
    rows = alleles.shape[0]
    all_high, all_mid, _ = split(alleles[...])
    toward = jnp.concatenate([all_high, all_mid], axis=0)
    prop = dot(toward, gap_high[...], 1, 1) + dot(toward, gap_low[...], 1, 1)
    prop = prop[:populations] + prop[rows : rows + populations]
    along = jnp.sum(mixture[:populations, :] * prop, axis=0, keepdims=True)
    stride = prop_ref.shape[0] * LANES // samples
    put_packed(prop_ref, 0, stride, prop + (twice_here[...] - along))
    if stride > populations:
        put_packed(prop_ref, populations, stride, twice_here[...])


def next_mixture(populations, mixture, twice_observed, prop_parts):
    rows, samples = mixture.shape
    stride = prop_parts[0].shape[0] * LANES // samples
    prop_sums = sum_packed(prop_parts, 0, stride, populations)
    if twice_observed is None:
        twice_observed = sum_packed(prop_parts, populations, stride, 1)
    moved = clip_unit(mixture[:populations] * prop_sums / twice_observed)
    return pad_rows(moved, rows), twice_observed


def next_alleles(populations, alleles, both_parts):
    alt_sums = sum_packed(both_parts, 0, 2 * populations, populations)
    ref_sums = sum_packed(both_parts, populations, 2 * populations, populations)
    current = alleles[:populations]
    weighted = current * alt_sums
    moved = clip_unit(weighted / (weighted + (1.0 - current) * ref_sums))
    return pad_rows(moved, alleles.shape[0])


def prepare_kernel(genotypes, observed, alt_out, ref_out, twice_out, landed, arrivals):
    samples, variants = genotypes.shape
    tall = samples // arrivals.shape[1]
    copies = []
    for index, top in enumerate(range(0, samples, tall)):
        here = pl.ds(top, tall)
        for place, source in enumerate((genotypes, observed)):
            copy = pltpu.make_async_copy(
                source.at[here, :], landed.at[place, here, :], arrivals.at[place, index]
            )
            copy.start()
            copies.append(copy)
    ones = jnp.ones((SUBLANES, variants), BF16)
    for index, top in enumerate(range(0, samples, tall)):
        here = slice(top, top + tall)
        copies[2 * index].wait()
        copies[2 * index + 1].wait()
        seen = landed[1, here, :].astype(F32)
        alt = seen * landed[0, here, :].astype(F32)
        alt_out[here, :] = alt
        ref_out[here, :] = 2.0 * seen - alt
        twice_out[:, here] = 2.0 * dot(ones, seen.astype(BF16), 1, 1)[:1]


def first_kernel(mixture, alleles, alt, ref, mixture_out, alleles_out, both_out, *refs):
    populations = mixture.shape[0]
    rows = mixture_out.shape[0]
    mix = pad_rows(mixture[...], rows)
    current = pad_rows(alleles[...], rows)
    mixture_out[...] = mix
    alleles_out[...] = current
    variant_sums(populations, mix, current, alt, ref, both_out, *refs)


def mixture_kernel(populations, with_twice, mixture, *refs):
    twice = refs[0][...] if with_twice else None
    prop_parts, outs = split_refs(refs[with_twice:], len(refs) - 2)
    mix, twice = next_mixture(populations, mixture[...], twice, prop_parts)
    outs[0][...] = mix
    if not with_twice:
        outs[1][...] = twice


def step_kernel(populations, mixture, alleles, *refs):
    both_parts, (alt, ref, alleles_out, both_out), refs = split_refs(refs, 2, 4)
    current = next_alleles(populations, alleles[...], both_parts)
    alleles_out[...] = current
    variant_sums(populations, mixture[...], current, alt, ref, both_out, *refs)


def split_refs(refs, *counts):
    groups = []
    for count in counts:
        groups.append(refs[:count])
        refs = refs[count:]
    return (*groups, refs)


def folded(values):
    squares = values * values
    tile = squares.reshape(-1, SUBLANES, squares.shape[1]).sum(axis=0)
    width = tile.shape[1]
    return sum(tile[:, i : i + LANES] for i in range(0, width, LANES))


def squares(zero, one, two, tile):
    step = one - zero
    tile[:SUBLANES, :] = folded(step)
    tile[SUBLANES:, :] = folded(two - one - step)


def mixture_square_kernel(populations, zero, one, twice, *refs):
    prop_parts, (two_out, tile) = split_refs(refs, len(refs) - 2)
    two, _ = next_mixture(populations, one[...], twice[...], prop_parts)
    two_out[...] = two
    squares(zero[...], one[...], two, tile)


def alleles_square_kernel(populations, zero, one, *refs):
    both_parts, (two_out, tile) = split_refs(refs, 2)
    two = next_alleles(populations, one[...], both_parts)
    two_out[...] = two
    squares(zero[...], one[...], two, tile)


def leap(zero, one, two, tile):
    first = jnp.sum(tile[:SUBLANES], axis=(0, 1), keepdims=True)
    second = jnp.sum(tile[SUBLANES:], axis=(0, 1), keepdims=True)
    alpha = jnp.maximum(1.0, jnp.sqrt(first / (second + NORM_EPS)))
    step = one - zero
    curve = two - one - step
    return zero + 2.0 * alpha * step + alpha * alpha * curve


def leap_kernel(populations, n_all, *refs):
    states = [ref[...] for ref in refs[:6]]
    mix_zero, all_zero, mix_one, all_one, mix_two, all_two = states
    mix_parts, all_parts, rest = split_refs(refs[6:], 2, n_all)
    alt, ref, mixture_out, alleles_out, both_out, *refs = rest
    mix_tile = mix_parts[0][...] + mix_parts[1][...]
    all_tile = pair_sum([part[...] for part in all_parts])
    clipped = row_mask(clip_unit(leap(mix_zero, mix_one, mix_two, mix_tile)), populations)
    mix = clipped / jnp.sum(clipped, axis=0, keepdims=True)
    current = row_mask(clip_unit(leap(all_zero, all_one, all_two, all_tile)), populations)
    mixture_out[...] = mix
    alleles_out[...] = current
    variant_sums(populations, mix, current, alt, ref, both_out, *refs)


def last_kernel(populations, mixture, alleles, *refs):
    both_parts, (mixture_out, alleles_out) = split_refs(refs, 2)
    mixture_out[...] = mixture[:populations, :]
    alleles_out[...] = next_alleles(populations, alleles[...], both_parts)[:populations]


def call(kernel, name, outs, args, scratch=(), flops=0):
    whole = pl.BlockSpec(memory_space=pltpu.VMEM)
    cost = pl.CostEstimate(flops=flops, bytes_accessed=0, transcendentals=0) if flops else None
    return pl.pallas_call(
        kernel,
        out_shape=tuple(jax.ShapeDtypeStruct(*out) for out in outs),
        in_specs=[pl.BlockSpec(memory_space=pltpu.VMEM)] * len(args),
        out_specs=(whole,) * len(outs),
        scratch_shapes=list(scratch),
        compiler_params=pltpu.CompilerParams(vmem_limit_bytes=VMEM_BYTES),
        cost_estimate=cost,
        name=name,
    )(*args)


def local(genotypes, observed, proportions, frequencies):
    populations, samples = proportions.shape
    variants = genotypes.shape[1]
    rows = -(-populations // 16) * 16
    state_out = (((rows, samples), F32), ((rows, variants), F32))
    packed = populations * samples // LANES
    both_out = ((2 * populations * variants // LANES, LANES), F32)
    sums_out = (both_out, ((samples, variants), BF16), ((samples, variants), BF16))
    tile_out = ((2 * SUBLANES, LANES), F32)
    turned = (pltpu.VMEM((samples, 6 * rows), BF16),)

    chunks = samples // blocks_of(samples, 128)
    flags, genotypes, observed = lax.optimization_barrier((gather_flags(), genotypes, observed))
    in_place = [
        pltpu.with_memory_space_constraint(array, pltpu.HBM) for array in (genotypes, observed)
    ]
    whole = pl.BlockSpec(memory_space=pltpu.VMEM)
    alt, ref, twice_here = pl.pallas_call(
        prepare_kernel,
        out_shape=(
            pltpu.VMEM((samples, variants), F32),
            pltpu.VMEM((samples, variants), F32),
            jax.ShapeDtypeStruct((1, samples), F32),
        ),
        in_specs=[pl.BlockSpec(memory_space=pltpu.HBM)] * 2,
        out_specs=(whole,) * 3,
        scratch_shapes=[
            pltpu.VMEM((2, samples, variants), jnp.int32),
            pltpu.SemaphoreType.DMA((2, chunks)),
        ],
        compiler_params=pltpu.CompilerParams(vmem_limit_bytes=VMEM_BYTES),
        name="prepare",
    )(*in_place)
    alleles = gather_frequencies(frequencies, flags)

    def sums(mixture, alleles, both, gaps, extra=0):
        (prop,) = call(
            functools.partial(sample_sums_kernel, populations),
            "sample_sums",
            (((packed + extra, LANES), F32),),
            (mixture, alleles, twice_here, *gaps),
        )
        both = both + swap(both, "samp", 1)
        return lax.optimization_barrier((prop, both))

    mix_zero, all_zero, both, *gaps = call(
        first_kernel,
        "first",
        (*state_out, *sums_out),
        (proportions, alleles, alt, ref),
        turned,
    )
    prop, both = sums(mix_zero, all_zero, both, gaps, samples // LANES)

    def moved_mixture(mixture, twice, prop):
        known = () if twice is None else (twice,)
        extra = () if known else (((1, samples), F32),)
        out = call(
            functools.partial(mixture_kernel, populations, len(known)),
            "mixture",
            (state_out[0], *extra),
            (mixture, *known, *all_parts_of(prop, "var")),
            flops=MIXTURE_COST,
        )
        return out[0], (known or out[1:])[0]

    def step(mixture, alleles, both):
        moved, both, *gaps = call(
            functools.partial(step_kernel, populations),
            "step",
            (state_out[1], *sums_out),
            (mixture, alleles, *parts_of(both, "samp", 1), alt, ref),
            turned,
        )
        return moved, *sums(mixture, moved, both, gaps)

    twice = None
    for repeat in range(STEPS):
        if repeat:
            mix_zero, twice = moved_mixture(mix_zero, twice, prop)
            all_zero, prop, both = step(mix_zero, all_zero, both)
        mix_one, twice = moved_mixture(mix_zero, twice, prop)
        all_one, prop, both = step(mix_one, all_zero, both)
        mix_two, mix_tile = call(
            functools.partial(mixture_square_kernel, populations),
            "mixture_square",
            (state_out[0], tile_out),
            (mix_zero, mix_one, twice, *all_parts_of(prop, "var")),
            flops=MIXTURE_COST,
        )
        all_two, all_tile = call(
            functools.partial(alleles_square_kernel, populations),
            "alleles_square",
            (state_out[1], tile_out),
            (all_zero, all_one, *parts_of(both, "samp", 1)),
            flops=ALLELES_COST,
        )
        mix_tile = mix_tile + swap(mix_tile, "samp", 1)
        mix_tile, all_tile = lax.optimization_barrier((mix_tile, all_tile))
        tiles = (*parts_of(mix_tile, "samp", 1), *all_parts_of(all_tile, "var"))
        mix_zero, all_zero, both, *gaps = call(
            functools.partial(leap_kernel, populations, len(tiles) - 2),
            "leap",
            (*state_out, *sums_out),
            (mix_zero, all_zero, mix_one, all_one, mix_two, all_two, *tiles, alt, ref),
            turned,
        )
        prop, both = sums(mix_zero, all_zero, both, gaps)
    mixture, _ = moved_mixture(mix_zero, twice, prop)
    return call(
        functools.partial(last_kernel, populations),
        "last",
        (((populations, samples), F32), ((populations, variants), F32)),
        (mixture, all_zero, *parts_of(both, "samp", 1)),
    )


def solution(mesh):
    placed = (P("samp", "var"), P("samp", "var"), P(None, "samp"), P(None, ("samp", "var")))
    return jax.shard_map(
        local,
        mesh=mesh,
        in_specs=placed,
        out_specs=(P(None, "samp"), P(None, "var")),
        check_vma=False,
    )
```
